128 devices in a mesh: seq: 16 (over y, x_lo, core), tensor: 8 (over z, x_hi).
Axes of the slice: x: 4 (x_hi: 2, x_lo: 2; x = x_hi * 2 + x_lo), y: 4, z: 4, core: 2. Of those that a mesh axis runs over, the one named last changes fastest.
Arguments:
- audio_codes: int32 [4096, 8], P('seq'), may hold values from 0 to 1023
- chroma_ids: int32 [4096], P('seq'), may hold values from 0 to 255
- song_ids: int32 [4096], P('seq'), may hold values from 0 to 3, never falling along the last dimension, each value on 1 to 2048 neighbouring positions
- code_table: bfloat16 [8, 1024, 4096], P(None, 'seq', 'tensor'), may hold values from -2.5 to 2.5
- chroma_table: bfloat16 [256, 4096], P(None, 'tensor'), may hold values from -2.5 to 2.5
- attention_gain: float32 [4096], replicated, may hold values from 0.1 to 1.9
- temporal_qkv: bfloat16 [3, 4096, 4096], P(None, None, 'tensor'), may hold values from -0.390625 to 0.390625
- temporal_out: bfloat16 [4096, 4096], P('tensor'), may hold values from -0.375 to 0.375
- output_gain: float32 [4096], replicated, may hold values from 0.1 to 1.9
- depth_input: bfloat16 [4096, 1024], P(None, 'tensor'), may hold values from -0.09375 to 0.09375
- depth_table: bfloat16 [7, 1024, 1024], P(None, None, 'tensor'), may hold values from -3 to 3
- depth_gain: float32 [1024], replicated, may hold values from 0.1 to 1.9
- depth_qkv: bfloat16 [3, 1024, 1024], P(None, None, 'tensor'), may hold values from -1.65625 to 1.65625
- depth_proj: bfloat16 [1024, 1024], P('tensor'), may hold values from -0.5 to 0.5
Outputs:
- temporal_hidden: bfloat16 [4096, 4096], P(('seq', 'tensor'))
- depth_hidden: bfloat16 [4096, 8, 1024], P(('seq', 'tensor'))
The draws below stay inside these ranges and needn't reach their ends.
All inputs are finite; a program needn't handle non-finite values.
Results may differ from the reference program's by a relative error of at most 0.029.
Values may be sent and summed in bfloat16 or wider, within the bound.
A program may use at most 192 MiB of HBM per device.

```python
import math
import jax
import jax.numpy as jnp
import numpy as np
from jax import lax

D = 4096
HEADS = 32
HEAD = 128
DD = 1024
DHEADS = 16
DHEAD = 64
BOOKS = 8
VOCAB = 1024
CHROMA = 256
SONGS = 4
FRAMES = 4096


def draw_temporal_qkv(key, part):
    key = jax.random.fold_in(key, 7)
    key_one = jax.random.fold_in(key, 0)
    stacked = jnp.clip(jax.random.normal(key_one, (3, D, D), jnp.float32), -4.0, 4.0)
    return (stacked * D ** (-0.5)).astype(jnp.bfloat16)


def draw_depth_qkv(key, part):
    key = jax.random.fold_in(key, 13)
    key_one = jax.random.fold_in(key, 0)
    stacked = jnp.clip(jax.random.normal(key_one, (3, DD, DD), jnp.float32), -4.0, 4.0)
    return (stacked * DD ** (-0.5)).astype(jnp.bfloat16)


def with_ends(array, stream_key, least, top_value):
    place = [jax.random.randint(jax.random.fold_in(stream_key, axis), (), 0, length) for axis, length in enumerate(array.shape)]
    main_axis = array.shape.index(max(array.shape))
    beside = place[:main_axis] + [(place[main_axis] + 1) % array.shape[main_axis]] + place[main_axis + 1:]
    return array.at[tuple(place)].set(least).at[tuple(beside)].set(top_value)


def shard_levels(own_key, extent, cuts, low, high):
    def one(position, shards_of):
        draws = jax.random.uniform(jax.random.fold_in(jax.random.fold_in(own_key, 6), position), (shards_of,), jnp.float32, low / len(cuts), high / len(cuts))
        return jnp.repeat(jnp.exp(draws), extent[position] // shards_of).reshape((-1,) + (1,) * (len(extent) - position - 1))

    gain = one(*cuts[0])
    for cut in cuts[1:]:
        gain = gain * one(*cut)
    return gain


def rank_bounds(count, lean):
    portions = [(1 << 20) // math.isqrt(standing ** lean) + 1 for standing in range(1, count + 1)]
    scale = 1 + sum(portions) // (1 << 30)
    return np.cumsum(np.array([max(1, weight // scale) for weight in portions]))


def ranked(rng, shape, number_of, slope):
    grid = rank_bounds(number_of, slope)
    ticket = jax.random.randint(jax.random.fold_in(rng, 1), shape, 0, int(grid[number_of - 1]))
    rank = jnp.searchsorted(jnp.asarray(grid, jnp.int32), ticket, side="right")
    return jax.random.permutation(jax.random.fold_in(rng, 2), number_of)[rank].astype(jnp.int32)


def profile(number_of, total, most, slope):
    loads = [(1 << 20) // math.isqrt(standing ** slope) + 1 for standing in range(2, number_of + 1)]
    rest, given = total - most - (number_of - 1), [1] * (number_of - 1)
    while rest > 0:
        movable = [i for i in range(number_of - 1) if given[i] < most]
        whole, left = sum([loads[i] for i in movable]), rest
        for i in movable:
            extra = min(most - given[i], max(1, left * loads[i] // whole), rest)
            given[i] = given[i] + extra
            rest = rest - extra
    return np.array([most] + given)


def ragged(rng, number_of, total, bound, lean):
    if number_of == 2:
        one = jax.random.randint(rng, (), max(1, total - bound), min(bound, total - 1) + 1)
        return jnp.stack([one, total - one])
    tallies = jnp.asarray(profile(number_of, total, bound, lean), jnp.int32)
    pairs = (number_of - 1) // 2
    giver, sink = tallies[1:1 + 2 * pairs:2], tallies[2:2 + 2 * pairs:2]
    slack = jnp.minimum(giver - 1, bound - sink)
    shifted = jax.random.randint(jax.random.fold_in(rng, 1), (pairs,), 0, 1 << 20) % (slack + 1)
    tallies = tallies.at[1:1 + 2 * pairs:2].set(giver - shifted).at[2:2 + 2 * pairs:2].set(sink + shifted)
    return tallies[jax.random.permutation(jax.random.fold_in(rng, 2), number_of)]


def normal_values(rng, dims, width, reach, shards=(), kind=jnp.bfloat16):
    drawn = jax.random.normal(rng, dims, jnp.float32) * width
    if len(shards) > 0:
        drawn = shard_levels(rng, dims, shards, -0.22, 0.18) * drawn
    return jnp.clip(drawn, min=-reach, max=reach).astype(kind)


def setup_inputs(seed: int = 0) -> dict:
    splits = jax.random.split(jax.random.key(seed), 15)
    audio_codes = with_ends(ranked(splits[0], (FRAMES, BOOKS), VOCAB, 1), jax.random.fold_in(splits[0], 3), 0, VOCAB - 1).astype(jnp.int32)
    chroma_ids = with_ends(ranked(splits[1], (FRAMES,), CHROMA, 2), jax.random.fold_in(splits[1], 3), 0, CHROMA - 1).astype(jnp.int32)
    song_ids = jnp.searchsorted(jnp.cumsum(ragged(splits[2], SONGS, FRAMES, FRAMES // 2, 2)), jnp.arange(FRAMES), side="right").astype(jnp.int32)
    code_table = normal_values(splits[3], (BOOKS, VOCAB, D), 0.2, 2.5, ((1, 16), (2, 8)))
    chroma_table = normal_values(splits[4], (CHROMA, D), 0.2, 2.5, ((1, 8),))
    attention_gain = jnp.clip(1.0 + 0.18 * jax.random.normal(splits[5], (D,), jnp.float32), 0.1, 1.9)
    temporal_qkv = draw_temporal_qkv(jax.random.fold_in(splits[14], 71), 0)
    temporal_out = normal_values(splits[7], (D, D), (D // 16) ** -0.5, 0.375, ((0, 8),))
    output_gain = jnp.clip(1.0 + 0.18 * jax.random.normal(splits[8], (D,), jnp.float32), 0.1, 1.9)
    depth_input = normal_values(splits[9], (D, DD), D ** -0.5, 0.09375, ((1, 8),))
    depth_table = normal_values(splits[10], (BOOKS - 1, VOCAB, DD), 0.5, 3.0, ((2, 8),))
    depth_gain = jnp.clip(1.0 + 0.18 * jax.random.normal(splits[11], (DD,), jnp.float32), 0.1, 1.9)
    depth_qkv = draw_depth_qkv(jax.random.fold_in(splits[14], 71), 0)
    depth_proj = normal_values(splits[13], (DD, DD), (DD // 8) ** -0.5, 0.5, ((0, 8),))
    return dict(audio_codes=audio_codes, chroma_ids=chroma_ids, song_ids=song_ids, code_table=code_table, chroma_table=chroma_table, attention_gain=attention_gain, temporal_qkv=temporal_qkv, temporal_out=temporal_out, output_gain=output_gain, depth_input=depth_input, depth_table=depth_table, depth_gain=depth_gain, depth_qkv=depth_qkv, depth_proj=depth_proj)


def rms_norm(entries, norm_gain):
    entries = entries.astype(jnp.float32)
    factor = lax.rsqrt(lax.optimization_barrier(jnp.mean(entries * entries, axis=-1, keepdims=True)) + 1e-05)
    return (entries * factor * norm_gain).astype(jnp.bfloat16)

def rotate(entries, positions):
    half_width = entries.shape[-1] // 2
    frequencies = 10000.0 ** (-(jnp.arange(half_width, dtype=jnp.float32) * 2.0 / entries.shape[-1]))
    angles = positions.astype(jnp.float32)[:, None] * frequencies[None, :]
    cosines = jnp.cos(angles)[:, None, :]
    sines = jnp.sin(angles)[:, None, :]
    leading = entries[..., :half_width]
    trailing = entries[..., half_width:]
    return jnp.concatenate([leading * cosines - trailing * sines, leading * sines + trailing * cosines], axis=-1)

def depth_attend(queries, keys_here, values_here):
    codebooks = queries.shape[1]
    scores = jnp.einsum('fqhd,fkhd->fhqk', queries.astype(jnp.float32), keys_here.astype(jnp.float32)) * queries.shape[3] ** (-0.5)
    ranks = jnp.arange(codebooks, dtype=jnp.int32)
    allowed = ranks[:, None] >= ranks[None, :]
    highest = lax.optimization_barrier(jnp.max(jnp.where(allowed, scores, -1e+30), axis=3, keepdims=True))
    weights = jnp.where(allowed, jnp.exp(scores - highest), 0.0)
    totals = lax.optimization_barrier(jnp.sum(weights, axis=3, keepdims=True))
    rounded = weights.astype(jnp.bfloat16)
    blended = jnp.einsum('fhqk,fkhd->fhqd', rounded.astype(jnp.float32), values_here.astype(jnp.float32)) / totals
    frames_here = queries.shape[0]
    return blended.transpose(0, 2, 1, 3).reshape(frames_here * codebooks, -1).astype(jnp.bfloat16)

def reference(audio_codes, chroma_ids, song_ids, code_table, chroma_table, attention_gain, temporal_qkv, temporal_out, output_gain, depth_input, depth_table, depth_gain, depth_qkv, depth_proj):
    embedded = jnp.zeros((FRAMES, D), jnp.float32)
    for codebook in range(BOOKS):
        embedded = embedded + jnp.take(code_table[codebook], audio_codes[:, codebook], axis=0).astype(jnp.float32)
    embedded = embedded + jnp.take(chroma_table, chroma_ids, axis=0).astype(jnp.float32)
    tokens = embedded.astype(jnp.bfloat16)
    normed = rms_norm(tokens, attention_gain)
    positions = jnp.arange(FRAMES, dtype=jnp.int32)
    queries = rotate(jnp.dot(normed, temporal_qkv[0], preferred_element_type=jnp.float32).reshape(FRAMES, HEADS, HEAD), positions).astype(jnp.bfloat16)
    keys_all = rotate(jnp.dot(normed, temporal_qkv[1], preferred_element_type=jnp.float32).reshape(FRAMES, HEADS, HEAD), positions).astype(jnp.bfloat16)
    values_all = jnp.dot(normed, temporal_qkv[2], preferred_element_type=jnp.float32).astype(jnp.bfloat16).reshape(FRAMES, HEADS, HEAD)
    allowed = (song_ids[:, None] == song_ids[None, :]) & (positions[:, None] >= positions[None, :])

    def one_head(parts):
        head_queries, head_keys, head_values = parts
        scores = jnp.dot(head_queries, head_keys.T, preferred_element_type=jnp.float32) * HEAD ** (-0.5)
        highest = lax.optimization_barrier(jnp.max(jnp.where(allowed, scores, -1e+30), axis=1, keepdims=True))
        weights = jnp.where(allowed, jnp.exp(scores - highest), 0.0)
        totals = lax.optimization_barrier(jnp.sum(weights, axis=1, keepdims=True))
        blended = jnp.dot(weights.astype(jnp.bfloat16), head_values, preferred_element_type=jnp.float32) / totals
        return blended.astype(jnp.bfloat16)
    per_head = lax.map(one_head, (queries.transpose(1, 0, 2), keys_all.transpose(1, 0, 2), values_all.transpose(1, 0, 2)))
    attended = per_head.transpose(1, 0, 2).reshape(FRAMES, D)
    temporal_hidden = (tokens.astype(jnp.float32) + jnp.dot(attended, temporal_out, preferred_element_type=jnp.float32)).astype(jnp.bfloat16)
    normed_hidden = rms_norm(temporal_hidden, output_gain)
    projected = jnp.dot(normed_hidden, depth_input, preferred_element_type=jnp.float32)
    lookups = jnp.stack([jnp.take(depth_table[codebook], audio_codes[:, codebook], axis=0) for codebook in range(BOOKS - 1)], axis=1).astype(jnp.float32)
    depth_inputs = jnp.concatenate([projected[:, None], projected[:, None] + lookups], axis=1).astype(jnp.bfloat16)
    flattened = depth_inputs.reshape(FRAMES * BOOKS, DD)
    depth_normed = rms_norm(flattened, depth_gain)
    depth_queries = jnp.dot(depth_normed, depth_qkv[0], preferred_element_type=jnp.float32).astype(jnp.bfloat16).reshape(FRAMES, BOOKS, DHEADS, DHEAD)
    depth_keys = jnp.dot(depth_normed, depth_qkv[1], preferred_element_type=jnp.float32).astype(jnp.bfloat16).reshape(FRAMES, BOOKS, DHEADS, DHEAD)
    depth_values = jnp.dot(depth_normed, depth_qkv[2], preferred_element_type=jnp.float32).astype(jnp.bfloat16).reshape(FRAMES, BOOKS, DHEADS, DHEAD)
    depth_mixed = depth_attend(depth_queries, depth_keys, depth_values)
    depth_hidden = (flattened.astype(jnp.float32) + jnp.dot(depth_mixed, depth_proj, preferred_element_type=jnp.float32)).astype(jnp.bfloat16)
    return (temporal_hidden, depth_hidden.reshape(FRAMES, BOOKS, DD))
```

```python
import functools

import jax
import jax.numpy as jnp
import numpy as np
from jax import lax
from jax.experimental import pallas as pl
from jax.experimental.pallas import tpu as pltpu
from jax.sharding import PartitionSpec as P

MESH = pl.DeviceIdType.MESH
F32 = jnp.float32
BF16 = jnp.bfloat16
HEAD = 128
DHEAD = 64
FR = 256
OWN = 32
PIECE = 2 * FR + 16


def rotation_tables():
    freq = 10000.0 ** (-(np.arange(64, dtype=np.float64) * 2.0 / HEAD))
    row = np.arange(FR, dtype=np.float64)[:, None] * freq[None]
    base = np.arange(16, dtype=np.float64)[:, None] * FR * freq[None]
    wide = lambda entries: np.concatenate([entries, entries], axis=1)
    rows = np.stack([wide(np.cos(row)), wide(np.sin(row))])
    bases = np.stack([wide(np.cos(base)), wide(np.sin(base))])
    return rows.astype(np.float32), bases.astype(np.float32)


def dot(a, b):
    return jnp.dot(a, b, preferred_element_type=F32)


def iota(shape, axis):
    return lax.broadcasted_iota(jnp.int32, shape, axis)


def kernel(
    pack_ref,
    gains_ref,
    rows_ref,
    bases_ref,
    ctab_ref,
    chroma_ref,
    wqkv_ref,
    wout_ref,
    din_ref,
    dtab_ref,
    dqkv_ref,
    dproj_ref,
    th_out,
    dh_out,
    wv,
    tab,
    hot,
    chroma,
    dtab,
    lk,
    lkf,
    cpb,
    colt,
    emb,
    psend,
    prec,
    toks,
    acc,
    kvs,
    kvb,
    qs,
    qb,
    sbuf,
    ob,
    att,
    rsend,
    rrec,
    thl,
    thb,
    di,
    pfull,
    prb,
    dq,
    dp,
    mixed,
    lsem,
    ysend,
    yrecv,
    rowsend,
    rowrecv,
    tsend,
    trecv,
):
    s = lax.axis_index("seq")
    t = lax.axis_index("tensor")
    y = s // 4
    x = (s // 2) % 2
    c = s % 2
    q4 = s % 4

    def ypeer(k):
        return (lax.rem(y + k, 4) * 4 + q4, t)

    sib = (y * 4 + x * 2 + (1 - c), t)
    xpeer = (y * 4 + (1 - x) * 2 + c, t)

    def tpeer(k):
        return (s, lax.rem(t + k, 8))

    def blk(k):
        return lax.rem(t + k, 8)

    def ring(r):
        return 2 * lax.rem(x + r // 2, 2) + lax.rem(c + r % 2, 2)

    counts = {"l": 0, "y": 0, "r": 0, "t": 0}
    pending = []

    def local(src, dst):
        n = counts["l"]
        counts["l"] += 1
        copy = pltpu.make_async_copy(src, dst, lsem.at[n])
        copy.start()
        return copy

    def remote(kind, src, dst, device):
        sends, recvs = {
            "y": (ysend, yrecv),
            "r": (rowsend, rowrecv),
            "t": (tsend, trecv),
        }[kind]
        n = counts[kind]
        counts[kind] += 1
        copy = pltpu.make_async_remote_copy(
            src_ref=src,
            dst_ref=dst,
            send_sem=sends.at[n],
            recv_sem=recvs.at[n],
            device_id=device,
            device_id_type=MESH,
        )
        copy.start()
        pending.append(copy)
        return copy

    load_dtab = local(dtab_ref, dtab)
    load_tab = local(ctab_ref, tab.at[:, 0])
    load_chroma = local(chroma_ref, chroma)
    load_w = local(wqkv_ref, wv)
    half = pl.ds(pl.multiple_of(512 * c, 512), 512)
    own_cols = pl.ds(pl.multiple_of(128 * t, 128), 128)
    load_dq = local(dqkv_ref.at[:, half], dq.at[:, half, own_cols])
    load_dp = local(
        dproj_ref.at[pl.ds(pl.multiple_of(64 * c, 64), 64)],
        dp.at[t, c],
    )
    di_half = pl.ds(pl.multiple_of(256 * c, 256), 256)
    load_di = local(
        din_ref.at[pl.ds(pl.multiple_of(512 * t + 256 * c, 256), 256)],
        di.at[di_half, own_cols],
    )

    barrier = pltpu.get_barrier_semaphore()
    greeted = [ypeer(k) for k in (1, 2, 3)] + [sib, xpeer] + [tpeer(k) for k in range(1, 8)]
    for device in greeted:
        pl.semaphore_signal(barrier, inc=1, device_id=device, device_id_type=MESH)
    pl.semaphore_wait(barrier, len(greeted))

    cpb[0] = pack_ref[...]
    code_copies = {k: remote("y", pack_ref, cpb.at[k], ypeer(k)) for k in (1, 2, 3)}
    chunk = lambda j: pl.ds(256 * j, 256)
    tab_x = [
        remote("r", ctab_ref.at[:, :, chunk(j)], tab.at[:, 2, :, chunk(j)], xpeer) for j in (0, 1)
    ]
    tab_s = [
        remote("r", ctab_ref.at[:, :, chunk(j)], tab.at[:, 1, :, chunk(j)], sib) for j in (0, 1)
    ]

    def send_di(k):
        return remote(
            "t",
            din_ref.at[pl.ds(pl.multiple_of(512 * blk(k) + 256 * c, 256), 256)],
            di.at[di_half, own_cols],
            tpeer(k),
        )

    def send_dq(i, k):
        return remote("t", dqkv_ref.at[i, half], dq.at[i, half, own_cols], tpeer(k))

    di_copies = [send_di(k) for k in range(1, 8)]
    dq_copies = {0: [send_dq(0, k) for k in range(1, 8)]}

    cpb_own = pack_ref[...].astype(F32)
    own_cols_t = jnp.transpose(cpb_own)
    colt[0] = own_cols_t
    load_dtab.wait()
    entry = iota((1, 1024), 1).astype(F32)
    for b in range(7):
        onehot = jnp.where(colt[0, :, b : b + 1] == entry, 1.0, 0.0).astype(BF16)
        lk[b] = dot(onehot, dtab[b]).astype(BF16)
    lk_copies = [
        remote(
            "t",
            lk.at[:, pl.ds(pl.multiple_of(OWN * blk(k), OWN), OWN)],
            lkf.at[:, :, own_cols],
            tpeer(k),
        )
        for k in range(1, 8)
    ]
    lkf[:, :, own_cols] = lk[:, pl.ds(pl.multiple_of(OWN * t, OWN), OWN)]

    lane = iota((1, 256), 1)
    lane_q = 2 * lax.rem(x + lane // 128, 2) + lax.rem(c + (lane // 64) % 2, 2)
    entry_row = (256 * y + 64 * lane_q + lane % 64).astype(F32)
    for k in (0, 1, 3, 2):
        if k:
            code_copies[k].wait_recv()
            colt[k] = jnp.transpose(cpb[k].astype(F32))
        for b in range(8):
            hot[k, :, 256 * b : 256 * (b + 1)] = jnp.where(
                colt[k, :, b : b + 1] == entry_row, 1.0, 0.0
            ).astype(BF16)
    load_tab.wait()

    part_copies = {}
    forwards = []
    for j in (0, 1):
        tab_x[j].wait_recv()
        forward = remote("r", tab.at[:, 2, :, chunk(j)], tab.at[:, 3, :, chunk(j)], sib)
        tab_s[j].wait_recv()
        forward.wait_recv()
        table = tab[:, :, :, 256 * j : 256 * (j + 1)].reshape(2048, 256)
        for k in (2, 1, 3, 0):
            part = dot(hot[k], table)
            if k == 0:
                emb[:, 256 * j : 256 * (j + 1)] = part
            else:
                psend[k, :, 256 * j : 256 * (j + 1)] = part.astype(BF16)
                part_copies[j, k] = remote(
                    "y", psend.at[k, :, chunk(j)], prec.at[4 - k, :, chunk(j)], ypeer(4 - k)
                )

    load_chroma.wait()
    chroma_hot = jnp.where(
        colt[0, :, 8:9] == iota((1, 256), 1).astype(F32), 1.0, 0.0
    ).astype(BF16)
    tok_copies = {}
    for j in (0, 1):
        cols = slice(256 * j, 256 * (j + 1))
        total = emb[:, cols] + dot(chroma_hot, chroma[:, cols])
        for k in (1, 3, 2):
            part_copies[j, k].wait_recv()
        for k in (1, 2, 3):
            total = total + prec[k, :, cols].astype(F32)
        toks[0, :, cols] = total.astype(BF16)
        for k in range(1, 8):
            tok_copies[j, k] = remote("t", toks.at[0, :, chunk(j)], toks.at[k, :, chunk(j)], tpeer(k))

    load_w.wait()
    ssq = jnp.zeros((FR, 1), F32)
    for n, k in enumerate((0, 1, 7, 2, 6, 3, 5, 4)):
        if k:
            tok_copies[0, k].wait_recv()
            tok_copies[1, k].wait_recv()
        feature = lax.rem(t + 8 - k, 8)
        block = toks[k].astype(F32)
        ssq = ssq + jnp.sum(block * block, axis=1, keepdims=True)
        gain = gains_ref[:, pl.ds(pl.multiple_of(512 * feature, 512), 512)]
        scaled = (block * gain).astype(BF16)
        for i in range(3):
            product = dot(scaled, wv[i, pl.ds(pl.multiple_of(512 * feature, 512), 512), :])
            if n == 0:
                acc[i] = product
            else:
                acc[i] += product
    dq_copies[1] = [send_dq(1, k) for k in range(1, 8)]
    dq_copies[2] = [send_dq(2, k) for k in range(1, 8)]
    dp_copies = [
        remote(
            "t",
            dproj_ref.at[pl.ds(pl.multiple_of(64 * c, 64), 64)],
            dp.at[t, c],
            tpeer(k),
        )
        for k in range(1, 8)
    ]

    factor = lax.rsqrt(ssq * (1.0 / 4096) + 1e-05)
    base_cos = bases_ref[0, pl.ds(s, 1), :]
    base_sin = bases_ref[1, pl.ds(s, 1), :]
    cosines = rows_ref[0] * base_cos - rows_ref[1] * base_sin
    sines = rows_ref[1] * base_cos + rows_ref[0] * base_sin
    sines = jnp.where(iota((1, HEAD), 1) < 64, -sines, sines)
    songs = pack_ref[9:10, :].astype(F32)
    song_row = iota((16, HEAD), 0)
    song_rows = jnp.where(
        song_row == 0, songs[:, :128], jnp.where(song_row == 1, songs[:, 128:], 0.0)
    ).astype(BF16)
    for h in range(4):
        cols = slice(HEAD * h, HEAD * (h + 1))
        for i in range(3):
            entries = acc[i, :, cols] * factor
            if i < 2:
                entries = entries * cosines + pltpu.roll(entries, 64, 1) * sines
            if i == 0:
                qs[h] = entries.astype(BF16)
            else:
                kvs[h, FR * (i - 1) : FR * i, :] = entries.astype(BF16)
        kvs[h, 2 * FR :, :] = song_rows

    load_wout = [
        local(wout_ref.at[:, pl.ds(512 * j, 512)], wv.at[0, pl.ds(512 * j, 512)]) for j in range(8)
    ]
    kv_copies = {}
    q_copies = {}
    for k in (1, 3, 2):
        head = lax.rem(y + k, 4)
        kv_copies[k] = remote("y", kvs.at[head], kvb.at[0, k], ypeer(k))
    for k in (1, 3, 2):
        head = lax.rem(y + k, 4)
        q_copies[k] = remote("y", qs.at[head], qb.at[k], ypeer(k))
    kvb[0, 0] = kvs[y]
    qb[0] = qs[y]
    kv_x = {}
    kv_s = {}
    for k in (0, 1, 3, 2):
        if k:
            kv_copies[k].wait_recv()
        kv_x[k] = remote("r", kvb.at[0, k], kvb.at[2, k], xpeer)
        kv_s[k] = remote("r", kvb.at[0, k], kvb.at[1, k], sib)
    kv_f = {}
    for k in (0, 1, 3, 2):
        kv_x[k].wait_recv()
        kv_f[k] = remote("r", kvb.at[2, k], kvb.at[3, k], sib)
    for k in (0, 1, 3, 2):
        kv_s[k].wait_recv()
        kv_f[k].wait_recv()
        if k:
            q_copies[k].wait_recv()

    scale = HEAD**-0.5
    row_id = iota((FR, 1), 0)
    col_id = iota((1, FR), 1)
    o_copies = {}
    for kq in (2, 1, 3, 0):
        yq = lax.rem(y + 4 - kq, 4)
        groups = jnp.minimum(yq + 1, 3)
        queries = qb[kq]
        query_song = colt[kq, :, 9:10]
        query_pos = FR * (4 * yq + q4) + row_id

        def scores_of(j, peak):
            yk = yq - j // 4
            r = j % 4
            kk = lax.rem(y + 4 - yk, 4)
            shard = 4 * yk + ring(r)
            tail = kvb[r, kk, 2 * FR :, :].astype(F32)
            key_song = jnp.concatenate([tail[0:1, :], tail[1:2, :]], axis=1)
            found = lax.dot_general(
                queries,
                kvb[r, kk, :FR, :],
                (((1,), (1,)), ((), ())),
                preferred_element_type=F32,
            )
            allowed = (query_song == key_song) & (query_pos >= FR * shard + col_id)
            found = jnp.where(allowed, found, -1e30)
            sbuf[j] = found
            return jnp.maximum(peak, jnp.max(found, axis=1, keepdims=True))

        peak = lax.fori_loop(0, 4 * groups, scores_of, jnp.full((FR, 1), -1e30, F32))

        def blend(j, carry):
            totals, blended = carry
            yk = yq - j // 4
            r = j % 4
            kk = lax.rem(y + 4 - yk, 4)
            weights = jnp.exp((sbuf[j] - peak) * scale)
            totals = totals + jnp.sum(weights, axis=1, keepdims=True)
            blended = blended + dot(weights.astype(BF16), kvb[r, kk, FR : 2 * FR, :])
            return totals, blended

        totals, blended = lax.fori_loop(
            0, 4 * groups, blend, (jnp.zeros((FR, 1), F32), jnp.zeros((FR, HEAD), F32))
        )
        head_cols = pl.ds(pl.multiple_of(HEAD * y, HEAD), HEAD)
        result = (blended / totals).astype(BF16)
        if kq:
            ob[kq] = result
            o_copies[kq] = remote("y", ob.at[kq], att.at[:, head_cols], ypeer(4 - kq))
        else:
            att[:, head_cols] = result
    for k in (1, 2, 3):
        o_copies[k].wait_recv()

    for copy in load_wout:
        copy.wait()
    attended = att[...]
    r_copies = {}
    for k in (4, 3, 5, 2, 6, 1, 7):
        columns = wv[0, pl.ds(pl.multiple_of(512 * blk(k), 512), 512), :]
        rsend[k] = dot(attended, columns).astype(BF16)
        r_copies[k] = remote("t", rsend.at[k], rrec.at[k], tpeer(k))
    total = toks[0].astype(F32) + dot(
        attended, wv[0, pl.ds(pl.multiple_of(512 * t, 512), 512), :]
    )
    emb[...] = total

    load_di.wait()
    load_dq.wait()
    load_dp.wait()
    for copy in di_copies:
        copy.wait_recv()
    di_forward = remote("r", di.at[di_half], di.at[di_half], sib)
    dq_forward = []
    for i in range(3):
        for copy in dq_copies[i]:
            copy.wait_recv()
        dq_forward.append(remote("r", dq.at[i, half], dq.at[i, half], sib))
    for copy in dp_copies:
        copy.wait_recv()
    dp_forward = remote("r", dp.at[:, c], dp.at[:, c], sib)

    for k in (1, 7, 2, 6, 3, 5, 4):
        r_copies[k].wait_recv()
        emb[...] += rrec[k].astype(F32)
    thl[...] = emb[...].astype(BF16)
    th_copies = [
        remote(
            "t",
            thl.at[pl.ds(pl.multiple_of(OWN * blk(k), OWN), OWN)],
            thb.at[:, pl.ds(pl.multiple_of(512 * t, 512), 512)],
            tpeer(k),
        )
        for k in range(1, 8)
    ]
    hidden = thl[...].astype(F32)
    square = jnp.sum(hidden * hidden, axis=1, keepdims=True)
    high = square.astype(BF16).astype(F32)
    middle = (square - high).astype(BF16).astype(F32)
    low = square - high - middle
    place = iota((FR, HEAD), 1)
    squares = jnp.where(
        place == 0, high, jnp.where(place == 1, middle, jnp.where(place == 2, low, 0.0))
    )
    pfull[:, :, 1024:] = squares.astype(BF16).reshape(8, OWN, HEAD)
    gain = gains_ref[:, pl.ds(pl.multiple_of(4096 + 512 * t, 512), 512)]
    scaled = (hidden * gain).astype(BF16)
    di_forward.wait_recv()
    for j in range(2):
        cols = slice(512 * j, 512 * (j + 1))
        pfull[:, :, cols] = dot(scaled, di[:, cols]).astype(BF16).reshape(8, OWN, 512)
    p_copies = [remote("t", pfull.at[blk(k)], prb.at[k], tpeer(k)) for k in range(1, 8)]
    thb[:, pl.ds(pl.multiple_of(512 * t, 512), 512)] = thl[
        pl.ds(pl.multiple_of(OWN * t, OWN), OWN), :
    ]

    summed = pfull[t].astype(F32)
    for copy in lk_copies:
        copy.wait_recv()
    for k in range(1, 8):
        p_copies[k - 1].wait_recv()
        summed = summed + prb[k].astype(F32)
    square = jnp.sum(summed[:, 1024:], axis=1, keepdims=True)
    projected = summed[:, :1024] * lax.rsqrt(square * (1.0 / 4096) + 1e-05)
    inputs = [projected.astype(BF16)]
    for b in range(7):
        inputs.append((projected + lkf[b].astype(F32)).astype(BF16))
    by_book = jnp.concatenate(inputs, axis=0)
    out_row = iota((FR, FR), 0)
    order = jnp.where(
        iota((FR, FR), 1) == (out_row % 8) * OWN + out_row // 8, 1.0, 0.0
    ).astype(BF16)
    inputs = dot(order, by_book)
    factor = lax.rsqrt(jnp.mean(inputs * inputs, axis=1, keepdims=True) + 1e-05)
    normed = (inputs * factor * gains_ref[:, 8192:]).astype(BF16)
    for copy in dq_forward:
        copy.wait_recv()
    depth_q, depth_k, depth_v = [dot(normed, dq[i]).astype(BF16) for i in range(3)]
    left = iota((1, 128), 1) < DHEAD
    seen_row = iota((256, 128), 0) % 128
    seen_col = iota((256, 128), 1)
    seen = (seen_col <= seen_row) & (seen_col >= (seen_row // 8) * 8)
    zero = jnp.zeros((), BF16)
    for p in range(8):
        cols = slice(128 * p, 128 * (p + 1))
        for g in range(2):
            rows = slice(128 * g, 128 * (g + 1))
            pair = depth_q[rows, cols]
            both = jnp.concatenate([jnp.where(left, pair, zero), jnp.where(left, zero, pair)], axis=0)
            found = lax.dot_general(
                both,
                depth_k[rows, cols],
                (((1,), (1,)), ((), ())),
                preferred_element_type=F32,
            )
            found = jnp.where(seen, found, -1e30)
            peak = jnp.max(found, axis=1, keepdims=True)
            weights = jnp.exp((found - peak) * DHEAD**-0.5)
            totals = jnp.sum(weights, axis=1, keepdims=True)
            blended = dot(weights.astype(BF16), depth_v[rows, cols]) / totals
            mixed[rows, cols] = jnp.where(left, blended[:128], blended[128:]).astype(BF16)
    dp_forward.wait_recv()
    dh_out[...] = (inputs + dot(mixed[...], dp[...].reshape(1024, 1024))).astype(BF16)

    for copy in th_copies:
        copy.wait_recv()
    th_out[...] = thb[...]
    for copy in pending:
        copy.wait_send()


def shards(
    audio_codes,
    chroma_ids,
    song_ids,
    code_table,
    chroma_table,
    attention_gain,
    temporal_qkv,
    temporal_out,
    output_gain,
    depth_input,
    depth_table,
    depth_gain,
    depth_qkv,
    depth_proj,
):
    pack = jnp.concatenate(
        [
            audio_codes.T,
            chroma_ids[None],
            song_ids[None],
            jnp.zeros((6, FR), jnp.int32),
        ],
        axis=0,
    )
    gains = jnp.concatenate([attention_gain, output_gain, depth_gain])[None]
    rows, bases = rotation_tables()
    vmem = pl.BlockSpec(memory_space=pltpu.VMEM)
    anywhere = pl.BlockSpec(memory_space=pl.ANY)
    temporal, depth = pl.pallas_call(
        kernel,
        out_shape=(
            jax.ShapeDtypeStruct((OWN, 4096), BF16),
            jax.ShapeDtypeStruct((FR, 1024), BF16),
        ),
        in_specs=[vmem] * 4 + [anywhere] * 8,
        out_specs=(vmem, vmem),
        scratch_shapes=[
            pltpu.VMEM((3, 4096, 512), BF16),
            pltpu.VMEM((8, 4, 64, 512), BF16),
            pltpu.VMEM((4, FR, 2048), BF16),
            pltpu.VMEM((256, 512), BF16),
            pltpu.VMEM((7, 1024, 128), BF16),
            pltpu.VMEM((7, FR, 128), BF16),
            pltpu.VMEM((7, OWN, 1024), BF16),
            pltpu.VMEM((4, 16, FR), jnp.int32),
            pltpu.VMEM((4, FR, 16), F32),
            pltpu.VMEM((FR, 512), F32),
            pltpu.VMEM((4, FR, 512), BF16),
            pltpu.VMEM((4, FR, 512), BF16),
            pltpu.VMEM((8, FR, 512), BF16),
            pltpu.VMEM((3, FR, 512), F32),
            pltpu.VMEM((4, PIECE, HEAD), BF16),
            pltpu.VMEM((4, 4, PIECE, HEAD), BF16),
            pltpu.VMEM((4, FR, HEAD), BF16),
            pltpu.VMEM((4, FR, HEAD), BF16),
            pltpu.VMEM((12, FR, FR), F32),
            pltpu.VMEM((4, FR, HEAD), BF16),
            pltpu.VMEM((FR, 512), BF16),
            pltpu.VMEM((8, FR, 512), BF16),
            pltpu.VMEM((8, FR, 512), BF16),
            pltpu.VMEM((FR, 512), BF16),
            pltpu.VMEM((OWN, 4096), BF16),
            pltpu.VMEM((512, 1024), BF16),
            pltpu.VMEM((8, OWN, 1152), BF16),
            pltpu.VMEM((8, OWN, 1152), BF16),
            pltpu.VMEM((3, 1024, 1024), BF16),
            pltpu.VMEM((8, 2, 64, 1024), BF16),
            pltpu.VMEM((FR, 1024), BF16),
            pltpu.SemaphoreType.DMA((15,)),
            pltpu.SemaphoreType.DMA((18,)),
            pltpu.SemaphoreType.DMA((18,)),
            pltpu.SemaphoreType.DMA((23,)),
            pltpu.SemaphoreType.DMA((23,)),
            pltpu.SemaphoreType.DMA((77,)),
            pltpu.SemaphoreType.DMA((77,)),
        ],
        compiler_params=pltpu.CompilerParams(
            collective_id=0, has_side_effects=True, vmem_limit_bytes=60 * 1024 * 1024
        ),
        name="layer",
    )(
        pack,
        gains,
        rows,
        bases,
        code_table,
        chroma_table,
        temporal_qkv,
        temporal_out,
        depth_input,
        depth_table,
        depth_qkv,
        depth_proj,
    )
    return temporal, depth.reshape(OWN, 8, 1024)


def solution(mesh):
    placed = (
        P("seq", None),
        P("seq"),
        P("seq"),
        P(None, "seq", "tensor"),
        P(None, "tensor"),
        P(),
        P(None, None, "tensor"),
        P("tensor", None),
        P(),
        P(None, "tensor"),
        P(None, None, "tensor"),
        P(),
        P(None, None, "tensor"),
        P("tensor", None),
    )
    return jax.shard_map(
        shards,
        mesh=mesh,
        in_specs=placed,
        out_specs=(P(("seq", "tensor"), None), P(("seq", "tensor"), None, None)),
        check_vma=False,
    )
```

```python
import functools

import jax
import jax.numpy as jnp
import numpy as np
from jax import lax
from jax.experimental import pallas as pl
from jax.experimental.pallas import tpu as pltpu
from jax.sharding import PartitionSpec as P

MESH = pl.DeviceIdType.MESH
F32 = jnp.float32
BF16 = jnp.bfloat16
HEAD = 128
DHEAD = 64
FR = 256
OWN = 32
PIECE = 2 * FR + 16


def rotation_tables():
    freq = 10000.0 ** (-(np.arange(64, dtype=np.float64) * 2.0 / HEAD))
    row = np.arange(FR, dtype=np.float64)[:, None] * freq[None]
    base = np.arange(16, dtype=np.float64)[:, None] * FR * freq[None]
    wide = lambda entries: np.concatenate([entries, entries], axis=1)
    rows = np.stack([wide(np.cos(row)), wide(np.sin(row))])
    bases = np.stack([wide(np.cos(base)), wide(np.sin(base))])
    return rows.astype(np.float32), bases.astype(np.float32)


def dot(a, b):
    return jnp.dot(a, b, preferred_element_type=F32)


def iota(shape, axis):
    return lax.broadcasted_iota(jnp.int32, shape, axis)


def kernel(
    codes_ref,
    chroma_ids_ref,
    songs_ref,
    again_ref,
    ogain_ref,
    dgain_ref,
    rows_ref,
    bases_ref,
    ctab_ref,
    chroma_ref,
    wqkv_ref,
    wout_ref,
    din_ref,
    dtab_ref,
    dqkv_ref,
    dproj_ref,
    th_out,
    dh_out,
    wv,
    tab,
    hot,
    chroma,
    dtab,
    lk,
    lkf,
    cpb,
    colt,
    emb,
    psend,
    prec,
    toks,
    acc,
    kvs,
    kvb,
    qs,
    qb,
    sbuf,
    ob,
    att,
    rsend,
    rrec,
    thl,
    thb,
    di,
    pfull,
    prb,
    dq,
    dp,
    mixed,
    lsem,
    ysend,
    yrecv,
    rowsend,
    rowrecv,
    tsend,
    trecv,
):
    s = lax.axis_index("seq")
    t = lax.axis_index("tensor")
    y = s // 4
    x = (s // 2) % 2
    c = s % 2
    q4 = s % 4

    def ypeer(k):
        return (lax.rem(y + k, 4) * 4 + q4, t)

    sib = (y * 4 + x * 2 + (1 - c), t)
    xpeer = (y * 4 + (1 - x) * 2 + c, t)

    def tpeer(k):
        return (s, lax.rem(t + k, 8))

    def blk(k):
        return lax.rem(t + k, 8)

    def ring(r):
        return 2 * lax.rem(x + r // 2, 2) + lax.rem(c + r % 2, 2)

    counts = {"l": 0, "y": 0, "r": 0, "t": 0}
    pending = []

    def local(src, dst):
        n = counts["l"]
        counts["l"] += 1
        copy = pltpu.make_async_copy(src, dst, lsem.at[n])
        copy.start()
        return copy

    def remote(kind, src, dst, device):
        sends, recvs = {
            "y": (ysend, yrecv),
            "r": (rowsend, rowrecv),
            "t": (tsend, trecv),
        }[kind]
        n = counts[kind]
        counts[kind] += 1
        copy = pltpu.make_async_remote_copy(
            src_ref=src,
            dst_ref=dst,
            send_sem=sends.at[n],
            recv_sem=recvs.at[n],
            device_id=device,
            device_id_type=MESH,
        )
        copy.start()
        pending.append(copy)
        return copy

    load_dtab = local(dtab_ref, dtab)
    load_tab = local(ctab_ref, tab.at[:, 0])
    load_chroma = local(chroma_ref, chroma)
    load_w = local(wqkv_ref, wv)
    own_cols = pl.ds(pl.multiple_of(128 * t, 128), 128)
    dq_half = pl.ds(pl.multiple_of(512 * c, 512), 512)
    dq_part = pl.ds(pl.multiple_of(512 * c + 128 * y, 128), 128)
    dp_part = pl.ds(pl.multiple_of(64 * c + 16 * y, 16), 16)
    di_half = pl.ds(pl.multiple_of(256 * c, 256), 256)
    di_part = pl.ds(pl.multiple_of(256 * c + 64 * y, 64), 64)

    def di_of(block):
        return din_ref.at[pl.ds(pl.multiple_of(512 * block + 256 * c + 64 * y, 64), 64)]

    load_dq = local(dqkv_ref.at[:, dq_part], dq.at[:, dq_part, own_cols])
    load_dp = local(dproj_ref.at[dp_part], dp.at[t, c, y])
    load_di = local(di_of(t), di.at[di_part, own_cols])

    cpb[0] = jnp.concatenate(
        [codes_ref[...], chroma_ids_ref[...], songs_ref[...], jnp.zeros((6, FR), jnp.int32)], axis=0
    )

    barrier = pltpu.get_barrier_semaphore()
    greeted = [ypeer(k) for k in (1, 2, 3)] + [sib, xpeer] + [tpeer(k) for k in range(1, 8)]
    for device in greeted:
        pl.semaphore_signal(barrier, inc=1, device_id=device, device_id_type=MESH)
    pl.semaphore_wait(barrier, len(greeted))

    code_copies = {k: remote("y", cpb.at[0], cpb.at[k], ypeer(k)) for k in (1, 2, 3)}
    chunk = lambda j: pl.ds(256 * j, 256)
    tab_x = [
        remote("r", ctab_ref.at[:, :, chunk(j)], tab.at[:, 2, :, chunk(j)], xpeer) for j in (0, 1)
    ]
    tab_s = [
        remote("r", ctab_ref.at[:, :, chunk(j)], tab.at[:, 1, :, chunk(j)], sib) for j in (0, 1)
    ]

    colt[0] = jnp.transpose(cpb[0].astype(F32))

    lane = iota((1, 256), 1)
    lane_q = 2 * lax.rem(x + lane // 128, 2) + lax.rem(c + (lane // 64) % 2, 2)
    entry_row = (256 * y + 64 * lane_q + lane % 64).astype(F32)
    for k in (0, 1, 3, 2):
        if k:
            code_copies[k].wait_recv()
            colt[k] = jnp.transpose(cpb[k].astype(F32))
        for b in range(8):
            hot[k, :, 256 * b : 256 * (b + 1)] = jnp.where(
                colt[k, :, b : b + 1] == entry_row, 1.0, 0.0
            ).astype(BF16)
    load_tab.wait()

    part_copies = {}
    for j in (0, 1):
        tab_x[j].wait_recv()
        forward = remote("r", tab.at[:, 2, :, chunk(j)], tab.at[:, 3, :, chunk(j)], sib)
        tab_s[j].wait_recv()
        forward.wait_recv()
        table = tab[:, :, :, 256 * j : 256 * (j + 1)].reshape(2048, 256)
        for k in (2, 1, 3, 0):
            part = dot(hot[k], table)
            if k == 0:
                emb[:, 256 * j : 256 * (j + 1)] = part
            else:
                psend[k, :, 256 * j : 256 * (j + 1)] = part.astype(BF16)
                part_copies[j, k] = remote(
                    "y", psend.at[k, :, chunk(j)], prec.at[4 - k, :, chunk(j)], ypeer(4 - k)
                )

    di_copies = [remote("t", di_of(blk(k)), di.at[di_part, own_cols], tpeer(k)) for k in range(1, 8)]
    dqa_copies = [
        remote("t", dqkv_ref.at[0:2, dq_part], dq.at[0:2, dq_part, own_cols], tpeer(k))
        for k in range(1, 8)
    ]

    load_chroma.wait()
    chroma_hot = jnp.where(
        colt[0, :, 8:9] == iota((1, 256), 1).astype(F32), 1.0, 0.0
    ).astype(BF16)
    tok_copies = {}
    for j in (0, 1):
        cols = slice(256 * j, 256 * (j + 1))
        total = emb[:, cols] + dot(chroma_hot, chroma[:, cols])
        for k in (1, 3, 2):
            part_copies[j, k].wait_recv()
        for k in (1, 2, 3):
            total = total + prec[k, :, cols].astype(F32)
        toks[0, :, cols] = total.astype(BF16)
        for k in range(1, 8):
            tok_copies[j, k] = remote("t", toks.at[0, :, chunk(j)], toks.at[k, :, chunk(j)], tpeer(k))

    load_dtab.wait()
    entry = iota((1, 1024), 1).astype(F32)
    for b in range(7):
        onehot = jnp.where(colt[0, :, b : b + 1] == entry, 1.0, 0.0).astype(BF16)
        lk[b] = dot(onehot, dtab[b]).astype(BF16)
    lkf[:, :, own_cols] = lk[:, pl.ds(pl.multiple_of(OWN * t, OWN), OWN)]

    load_di.wait()
    load_dq.wait()
    for copy in di_copies:
        copy.wait_recv()
    di_y = [remote("y", di.at[di_part], di.at[di_part], ypeer(k)) for k in (1, 3, 2)]
    for copy in dqa_copies:
        copy.wait_recv()
    dqa_y = [
        remote("y", dq.at[0:2, dq_part], dq.at[0:2, dq_part], ypeer(k)) for k in (1, 3, 2)
    ]

    load_w.wait()
    ssq = jnp.zeros((FR, 1), F32)
    for n, k in enumerate((0, 1, 7, 2, 6, 3, 5, 4)):
        if k:
            tok_copies[0, k].wait_recv()
            tok_copies[1, k].wait_recv()
        feature = lax.rem(t + 8 - k, 8)
        block = toks[k].astype(F32)
        ssq = ssq + jnp.sum(block * block, axis=1, keepdims=True)
        gain = again_ref[:, pl.ds(pl.multiple_of(512 * feature, 512), 512)]
        scaled = (block * gain).astype(BF16)
        for i in range(3):
            product = dot(scaled, wv[i, pl.ds(pl.multiple_of(512 * feature, 512), 512), :])
            if n == 0:
                acc[i] = product
            else:
                acc[i] += product
    factor = lax.rsqrt(ssq * (1.0 / 4096) + 1e-05)
    base_cos = bases_ref[0, pl.ds(s, 1), :]
    base_sin = bases_ref[1, pl.ds(s, 1), :]
    cosines = rows_ref[0] * base_cos - rows_ref[1] * base_sin
    sines = rows_ref[1] * base_cos + rows_ref[0] * base_sin
    sines = jnp.where(iota((1, HEAD), 1) < 64, -sines, sines)
    songs = songs_ref[...].astype(F32)
    song_row = iota((16, HEAD), 0)
    song_rows = jnp.where(
        song_row == 0, songs[:, :128], jnp.where(song_row == 1, songs[:, 128:], 0.0)
    ).astype(BF16)
    for h in range(4):
        cols = slice(HEAD * h, HEAD * (h + 1))
        for i in range(3):
            entries = acc[i, :, cols] * factor
            if i < 2:
                entries = entries * cosines + pltpu.roll(entries, 64, 1) * sines
            if i == 0:
                qs[h] = entries.astype(BF16)
            else:
                kvs[h, FR * (i - 1) : FR * i, :] = entries.astype(BF16)
        kvs[h, 2 * FR :, :] = song_rows

    load_wout = [
        local(wout_ref.at[:, pl.ds(512 * j, 512)], wv.at[0, pl.ds(512 * j, 512)]) for j in range(8)
    ]
    kv_copies = {}
    q_copies = {}
    for k in (1, 3, 2):
        head = lax.rem(y + k, 4)
        kv_copies[k] = remote("y", kvs.at[head], kvb.at[0, k], ypeer(k))
    for k in (1, 3, 2):
        head = lax.rem(y + k, 4)
        q_copies[k] = remote("y", qs.at[head], qb.at[k], ypeer(k))
    kvb[0, 0] = kvs[y]
    qb[0] = qs[y]
    kv_x = {}
    kv_s = {}
    for k in (0, 1, 3, 2):
        if k:
            kv_copies[k].wait_recv()
        kv_x[k] = remote("r", kvb.at[0, k], kvb.at[2, k], xpeer)
        kv_s[k] = remote("r", kvb.at[0, k], kvb.at[1, k], sib)
    kv_f = {}
    for k in (0, 1, 3, 2):
        kv_x[k].wait_recv()
        kv_f[k] = remote("r", kvb.at[2, k], kvb.at[3, k], sib)
    for k in (0, 1, 3, 2):
        kv_s[k].wait_recv()
        kv_f[k].wait_recv()
        if k:
            q_copies[k].wait_recv()

    lk_copies = [
        remote(
            "t",
            lk.at[:, pl.ds(pl.multiple_of(OWN * blk(k), OWN), OWN)],
            lkf.at[:, :, own_cols],
            tpeer(k),
        )
        for k in range(1, 8)
    ]
    dqb_copies = [
        remote("t", dqkv_ref.at[2, dq_part], dq.at[2, dq_part, own_cols], tpeer(k))
        for k in range(1, 8)
    ]
    dp_copies = [remote("t", dproj_ref.at[dp_part], dp.at[t, c, y], tpeer(k)) for k in range(1, 8)]

    scale = HEAD**-0.5 * float(np.log2(np.e))
    behind = iota((FR, FR), 1) - iota((FR, FR), 0)
    o_copies = {}
    for kq in (2, 1, 3, 0):
        yq = lax.rem(y + 4 - kq, 4)
        earlier = jnp.minimum(yq, 2)
        queries = qb[kq]
        query_song = jnp.broadcast_to(colt[kq, :, 9:10], (FR, HEAD))

        def scores_of(group, r, kk, same_row):
            tail = kvb[r, kk, 2 * FR :, :].astype(F32)
            found = lax.dot_general(
                queries,
                kvb[r, kk, :FR, :],
                (((1,), (1,)), ((), ())),
                preferred_element_type=F32,
            )
            allowed = jnp.concatenate(
                [query_song == tail[0:1, :], query_song == tail[1:2, :]], axis=1
            )
            if same_row:
                allowed = allowed & (behind <= FR * (q4 - ring(r)))
            found = jnp.where(allowed, found, -1e30)
            sbuf[4 * group + r] = found
            return jnp.maximum(found[:, :HEAD], found[:, HEAD:])

        def highest_of(group, highest, same_row):
            kk = lax.rem(kq + group, 4)
            for r in range(4):
                highest = jnp.maximum(highest, scores_of(group, r, kk, same_row))
            return highest

        highest = highest_of(0, jnp.full((FR, HEAD), -1e30, F32), True)
        highest = lax.fori_loop(
            1, earlier + 1, lambda group, carry: highest_of(group, carry, False), highest
        )
        peak = jnp.max(highest, axis=1, keepdims=True) * scale

        def blend(group, carry):
            totals, blended = carry
            kk = lax.rem(kq + group, 4)
            for r in range(4):
                weights = jnp.exp2(sbuf[4 * group + r] * scale - peak)
                totals = totals + (weights[:, :HEAD] + weights[:, HEAD:])
                blended = blended + dot(weights.astype(BF16), kvb[r, kk, FR : 2 * FR, :])
            return totals, blended

        totals, blended = lax.fori_loop(
            0, earlier + 1, blend, (jnp.zeros((FR, HEAD), F32), jnp.zeros((FR, HEAD), F32))
        )
        totals = jnp.sum(totals, axis=1, keepdims=True)
        head_cols = pl.ds(pl.multiple_of(HEAD * y, HEAD), HEAD)
        result = (blended / totals).astype(BF16)
        if kq:
            ob[kq] = result
            o_copies[kq] = remote("y", ob.at[kq], att.at[:, head_cols], ypeer(4 - kq))
        else:
            att[:, head_cols] = result
    for k in (1, 2, 3):
        o_copies[k].wait_recv()

    for copy in load_wout:
        copy.wait()
    attended = att[...]
    r_copies = {}
    for k in (4, 3, 5, 2, 6, 1, 7):
        columns = wv[0, pl.ds(pl.multiple_of(512 * blk(k), 512), 512), :]
        rsend[k] = dot(attended, columns).astype(BF16)
        r_copies[k] = remote("t", rsend.at[k], rrec.at[k], tpeer(k))
    total = toks[0].astype(F32) + dot(
        attended, wv[0, pl.ds(pl.multiple_of(512 * t, 512), 512), :]
    )
    emb[...] = total

    load_dp.wait()
    for copy in dqb_copies + dp_copies:
        copy.wait_recv()
    dqb_y = [remote("y", dq.at[2, dq_part], dq.at[2, dq_part], ypeer(k)) for k in (1, 3, 2)]
    dp_y = [remote("y", dp.at[:, c, y], dp.at[:, c, y], ypeer(k)) for k in (1, 3, 2)]
    for copy in di_y:
        copy.wait_recv()
    di_forward = remote("r", di.at[di_half], di.at[di_half], sib)
    for copy in dqa_y:
        copy.wait_recv()
    dqa_forward = remote("r", dq.at[0:2, dq_half], dq.at[0:2, dq_half], sib)

    for k in (1, 7, 2, 6, 3, 5, 4):
        r_copies[k].wait_recv()
        emb[...] += rrec[k].astype(F32)
    thl[...] = emb[...].astype(BF16)
    hidden = thl[...].astype(F32)
    square = jnp.sum(hidden * hidden, axis=1, keepdims=True)
    high = square.astype(BF16).astype(F32)
    middle = (square - high).astype(BF16).astype(F32)
    low = square - high - middle
    place = iota((FR, HEAD), 1)
    squares = jnp.where(
        place == 0, high, jnp.where(place == 1, middle, jnp.where(place == 2, low, 0.0))
    )
    pfull[:, :, 1024:] = squares.astype(BF16).reshape(8, OWN, HEAD)
    gain = ogain_ref[:, pl.ds(pl.multiple_of(512 * t, 512), 512)]
    scaled = (hidden * gain).astype(BF16)
    di_forward.wait_recv()
    for j in range(2):
        cols = slice(512 * j, 512 * (j + 1))
        pfull[:, :, cols] = dot(scaled, di[:, cols]).astype(BF16).reshape(8, OWN, 512)
    p_copies = [remote("t", pfull.at[blk(k)], prb.at[k], tpeer(k)) for k in range(1, 8)]
    th_copies = [
        remote(
            "t",
            thl.at[pl.ds(pl.multiple_of(OWN * blk(k), OWN), OWN)],
            thb.at[:, pl.ds(pl.multiple_of(512 * t, 512), 512)],
            tpeer(k),
        )
        for k in range(1, 8)
    ]
    thb[:, pl.ds(pl.multiple_of(512 * t, 512), 512)] = thl[
        pl.ds(pl.multiple_of(OWN * t, OWN), OWN), :
    ]

    for copy in dqb_y:
        copy.wait_recv()
    dqb_forward = remote("r", dq.at[2, dq_half], dq.at[2, dq_half], sib)
    for copy in dp_y:
        copy.wait_recv()
    dp_forward = remote("r", dp.at[:, c], dp.at[:, c], sib)

    summed = pfull[t].astype(F32)
    for copy in lk_copies:
        copy.wait_recv()
    for k in range(1, 8):
        p_copies[k - 1].wait_recv()
        summed = summed + prb[k].astype(F32)
    square = jnp.sum(summed[:, 1024:], axis=1, keepdims=True)
    projected = summed[:, :1024] * lax.rsqrt(square * (1.0 / 4096) + 1e-05)
    inputs = [projected.astype(BF16)]
    for b in range(7):
        inputs.append((projected + lkf[b].astype(F32)).astype(BF16))
    by_book = jnp.concatenate(inputs, axis=0)
    out_row = iota((FR, FR), 0)
    order = jnp.where(
        iota((FR, FR), 1) == (out_row % 8) * OWN + out_row // 8, 1.0, 0.0
    ).astype(BF16)
    inputs = dot(order, by_book)
    factor = lax.rsqrt(jnp.mean(inputs * inputs, axis=1, keepdims=True) + 1e-05)
    normed = (inputs * factor * dgain_ref[...]).astype(BF16)
    dqa_forward.wait_recv()
    dqb_forward.wait_recv()
    depth_q, depth_k, depth_v = [dot(normed, dq[i]).astype(BF16) for i in range(3)]
    left = iota((1, 128), 1) < DHEAD
    seen_row = iota((256, 128), 0) % 128
    seen_col = iota((256, 128), 1)
    seen = (seen_col <= seen_row) & (seen_col >= (seen_row // 8) * 8)
    zero = jnp.zeros((), BF16)
    for p in range(8):
        cols = slice(128 * p, 128 * (p + 1))
        for g in range(2):
            rows = slice(128 * g, 128 * (g + 1))
            pair = depth_q[rows, cols]
            both = jnp.concatenate([jnp.where(left, pair, zero), jnp.where(left, zero, pair)], axis=0)
            found = lax.dot_general(
                both,
                depth_k[rows, cols],
                (((1,), (1,)), ((), ())),
                preferred_element_type=F32,
            )
            found = jnp.where(seen, found, -1e30)
            peak = jnp.max(found, axis=1, keepdims=True)
            weights = jnp.exp((found - peak) * DHEAD**-0.5)
            totals = jnp.sum(weights, axis=1, keepdims=True)
            blended = dot(weights.astype(BF16), depth_v[rows, cols]) / totals
            mixed[rows, cols] = jnp.where(left, blended[:128], blended[128:]).astype(BF16)
    dp_forward.wait_recv()
    dh_out[...] = (inputs + dot(mixed[...], dp[...].reshape(1024, 1024))).astype(BF16)

    for copy in th_copies:
        copy.wait_recv()
    th_out[...] = thb[...]
    for copy in pending:
        copy.wait_send()


def shards(
    audio_codes,
    chroma_ids,
    song_ids,
    code_table,
    chroma_table,
    attention_gain,
    temporal_qkv,
    temporal_out,
    output_gain,
    depth_input,
    depth_table,
    depth_gain,
    depth_qkv,
    depth_proj,
):
    rows, bases = rotation_tables()
    vmem = pl.BlockSpec(memory_space=pltpu.VMEM)
    anywhere = pl.BlockSpec(memory_space=pl.ANY)
    temporal, depth = pl.pallas_call(
        kernel,
        out_shape=(
            jax.ShapeDtypeStruct((OWN, 4096), BF16),
            jax.ShapeDtypeStruct((FR, 1024), BF16),
        ),
        in_specs=[vmem] * 8 + [anywhere] * 8,
        out_specs=(vmem, vmem),
        scratch_shapes=[
            pltpu.VMEM((3, 4096, 512), BF16),
            pltpu.VMEM((8, 4, 64, 512), BF16),
            pltpu.VMEM((4, FR, 2048), BF16),
            pltpu.VMEM((256, 512), BF16),
            pltpu.VMEM((7, 1024, 128), BF16),
            pltpu.VMEM((7, FR, 128), BF16),
            pltpu.VMEM((7, OWN, 1024), BF16),
            pltpu.VMEM((4, 16, FR), jnp.int32),
            pltpu.VMEM((4, FR, 16), F32),
            pltpu.VMEM((FR, 512), F32),
            pltpu.VMEM((4, FR, 512), BF16),
            pltpu.VMEM((4, FR, 512), BF16),
            pltpu.VMEM((8, FR, 512), BF16),
            pltpu.VMEM((3, FR, 512), F32),
            pltpu.VMEM((4, PIECE, HEAD), BF16),
            pltpu.VMEM((4, 4, PIECE, HEAD), BF16),
            pltpu.VMEM((4, FR, HEAD), BF16),
            pltpu.VMEM((4, FR, HEAD), BF16),
            pltpu.VMEM((12, FR, FR), F32),
            pltpu.VMEM((4, FR, HEAD), BF16),
            pltpu.VMEM((FR, 512), BF16),
            pltpu.VMEM((8, FR, 512), BF16),
            pltpu.VMEM((8, FR, 512), BF16),
            pltpu.VMEM((FR, 512), BF16),
            pltpu.VMEM((OWN, 4096), BF16),
            pltpu.VMEM((512, 1024), BF16),
            pltpu.VMEM((8, OWN, 1152), BF16),
            pltpu.VMEM((8, OWN, 1152), BF16),
            pltpu.VMEM((3, 1024, 1024), BF16),
            pltpu.VMEM((8, 2, 4, 16, 1024), BF16),
            pltpu.VMEM((FR, 1024), BF16),
            pltpu.SemaphoreType.DMA((15,)),
            pltpu.SemaphoreType.DMA((30,)),
            pltpu.SemaphoreType.DMA((30,)),
            pltpu.SemaphoreType.DMA((22,)),
            pltpu.SemaphoreType.DMA((22,)),
            pltpu.SemaphoreType.DMA((77,)),
            pltpu.SemaphoreType.DMA((77,)),
        ],
        compiler_params=pltpu.CompilerParams(
            collective_id=0, has_side_effects=True, vmem_limit_bytes=60 * 1024 * 1024
        ),
        name="layer",
    )(
        audio_codes.T,
        chroma_ids[None],
        song_ids[None],
        attention_gain[None],
        output_gain[None],
        depth_gain[None],
        rows,
        bases,
        code_table,
        chroma_table,
        temporal_qkv,
        temporal_out,
        depth_input,
        depth_table,
        depth_qkv,
        depth_proj,
    )
    return temporal, depth.reshape(OWN, 8, 1024)


def solution(mesh):
    placed = (
        P("seq", None),
        P("seq"),
        P("seq"),
        P(None, "seq", "tensor"),
        P(None, "tensor"),
        P(),
        P(None, None, "tensor"),
        P("tensor", None),
        P(),
        P(None, "tensor"),
        P(None, None, "tensor"),
        P(),
        P(None, None, "tensor"),
        P("tensor", None),
    )
    return jax.shard_map(
        shards,
        mesh=mesh,
        in_specs=placed,
        out_specs=(P(("seq", "tensor"), None), P(("seq", "tensor"), None, None)),
        check_vma=False,
    )
```

```python
import functools

import jax
import jax.numpy as jnp
import numpy as np
from jax import lax
from jax.experimental import pallas as pl
from jax.experimental.pallas import tpu as pltpu
from jax.sharding import PartitionSpec as P

MESH = pl.DeviceIdType.MESH
F32 = jnp.float32
BF16 = jnp.bfloat16
HEAD = 128
DHEAD = 64
FR = 256
OWN = 32
HR = FR // 2
HALF = OWN // 2
PIECE = 3 * HR + 16


def rotation_tables():
    freq = 10000.0 ** (-(np.arange(64, dtype=np.float64) * 2.0 / HEAD))
    frames = np.arange(FR, dtype=np.float64).reshape(8, 2, HALF).transpose(1, 0, 2).reshape(FR)
    row = frames[:, None] * freq[None]
    base = np.arange(16, dtype=np.float64)[:, None] * FR * freq[None]
    wide = lambda entries: np.concatenate([entries, entries], axis=1)
    rows = np.stack([wide(np.cos(row)), wide(np.sin(row))])
    bases = np.stack([wide(np.cos(base)), wide(np.sin(base))])
    return rows.astype(np.float32), bases.astype(np.float32)


def dot(a, b):
    return jnp.dot(a, b, preferred_element_type=F32)


def iota(shape, axis):
    return lax.broadcasted_iota(jnp.int32, shape, axis)


def kernel(
    codes_ref,
    chroma_ids_ref,
    songs_ref,
    again_ref,
    ogain_ref,
    dgain_ref,
    rows_ref,
    bases_ref,
    ctab_ref,
    chroma_ref,
    wqkv_ref,
    wout_ref,
    din_ref,
    dtab_ref,
    dqkv_ref,
    dproj_ref,
    th_out,
    dh_out,
    wv,
    tab,
    hot,
    chroma,
    dtab,
    lk,
    lkf,
    cpb,
    colt,
    emb,
    resid,
    psend,
    prec,
    toks,
    acc,
    kvs,
    kvb,
    sbuf,
    ob,
    att,
    rsend,
    rrec,
    thl,
    thb,
    di,
    pfull,
    prb,
    dq,
    dp,
    mixed,
    lsem,
    ysend,
    yrecv,
    rowsend,
    rowrecv,
    tsend,
    trecv,
):
    s = lax.axis_index("seq")
    t = lax.axis_index("tensor")
    y = s // 4
    x = (s // 2) % 2
    c = s % 2
    q4 = s % 4

    def ypeer(k):
        return (lax.rem(y + k, 4) * 4 + q4, t)

    sib = (y * 4 + x * 2 + (1 - c), t)
    xpeer = (y * 4 + (1 - x) * 2 + c, t)

    def tpeer(k):
        return (s, lax.rem(t + k, 8))

    def blk(k):
        return lax.rem(t + k, 8)

    def ring(r):
        return 2 * lax.rem(x + r // 2, 2) + lax.rem(c + r % 2, 2)

    counts = {"l": 0, "y": 0, "r": 0, "t": 0}
    pending = []
    left_already = []

    def leave(*copies):
        for copy in copies:
            copy.wait_send()
            left_already.append(copy)

    def local(src, dst):
        n = counts["l"]
        counts["l"] += 1
        copy = pltpu.make_async_copy(src, dst, lsem.at[n])
        copy.start()
        return copy

    def remote(kind, src, dst, device):
        sends, recvs = {
            "y": (ysend, yrecv),
            "r": (rowsend, rowrecv),
            "t": (tsend, trecv),
        }[kind]
        n = counts[kind]
        counts[kind] += 1
        copy = pltpu.make_async_remote_copy(
            src_ref=src,
            dst_ref=dst,
            send_sem=sends.at[n],
            recv_sem=recvs.at[n],
            device_id=device,
            device_id_type=MESH,
        )
        copy.start()
        pending.append(copy)
        return copy

    z = t // 2
    xh = t % 2

    def zpeer(k):
        return (s, 2 * lax.rem(z + k, 4) + xh)

    hpeer = (s, 2 * z + 1 - xh)
    load_tab = local(ctab_ref, tab.at[:, 0])
    load_chroma = local(chroma_ref, chroma)
    own_cols = pl.ds(pl.multiple_of(128 * t, 128), 128)
    dq_half = pl.ds(pl.multiple_of(512 * c, 512), 512)
    dq_part = pl.ds(pl.multiple_of(512 * c + 128 * y, 128), 128)
    dp_half = pl.ds(pl.multiple_of(64 * c, 64), 64)
    di_half = pl.ds(pl.multiple_of(256 * c, 256), 256)
    di_part = pl.ds(pl.multiple_of(256 * c + 64 * y, 64), 64)

    def di_of(block):
        return din_ref.at[pl.ds(pl.multiple_of(512 * block + 256 * c + 64 * y, 64), 64)]

    load_di = local(di_of(t), di.at[di_part, own_cols])
    load_weights = [
        local(dqkv_ref.at[0:2, dq_part], dq.at[0:2, dq_part, own_cols]),
        local(dqkv_ref.at[2, dq_half], dq.at[2, dq_half, own_cols]),
        local(dproj_ref.at[dp_half], dp.at[t, c]),
    ]


    cpb[0] = jnp.concatenate(
        [codes_ref[...], chroma_ids_ref[...], songs_ref[...], jnp.zeros((6, FR), jnp.int32)], axis=0
    )

    barrier = pltpu.get_barrier_semaphore()
    greeted = [ypeer(k) for k in (1, 2, 3)] + [sib, xpeer] + [tpeer(k) for k in range(1, 8)]
    for device in greeted:
        pl.semaphore_signal(barrier, inc=1, device_id=device, device_id_type=MESH)
    def to_columns(k):
        columns = jnp.transpose(cpb[k].astype(F32))
        colt[k] = jnp.concatenate(
            [
                columns[OWN * o + HALF * h : OWN * o + HALF * (h + 1)]
                for h in range(2)
                for o in range(8)
            ],
            axis=0,
        )

    lane = iota((1, 256), 1)
    lane_q = 2 * lax.rem(x + lane // 128, 2) + lax.rem(c + (lane // 64) % 2, 2)
    entry_row = (256 * y + 64 * lane_q + lane % 64).astype(F32)
    def encode(k):
        to_columns(k)
        for b in range(8):
            hot[k, :, 256 * b : 256 * (b + 1)] = jnp.where(
                colt[k, :, b : b + 1] == entry_row, 1.0, 0.0
            ).astype(BF16)

    encode(0)
    load_chroma.wait()
    chroma_hot = jnp.where(
        colt[0, :, 8:9] == iota((1, 256), 1).astype(F32), 1.0, 0.0
    ).astype(BF16)
    emb[...] = dot(chroma_hot, chroma[...])

    for copy in load_weights:
        copy.wait()
    load_tab.wait()
    pl.semaphore_wait(barrier, len(greeted))

    starts = (0, 128, 256, 384, 512)
    chunk = lambda j: pl.ds(starts[j], starts[j + 1] - starts[j])
    code_copies = {k: remote("y", cpb.at[0], cpb.at[k], ypeer(k)) for k in (1, 3, 2)}
    tab_x = []

    def next_table():
        j = len(tab_x)
        if j:
            leave(tab_x[-1])
        tab_x.append(
            remote("r", tab.at[:, 0, :, chunk(j)], tab.at[:, 2, :, chunk(j)], xpeer)
        )

    next_table()
    tab_s = remote("r", tab.at[:, 0], tab.at[:, 1], sib)

    def weights_at(block):
        cols = pl.ds(pl.multiple_of(128 * block, 128), 128)
        return (dq.at[0:2, dq_part, cols], dq.at[2, dq_half, cols], dp.at[block, c])

    def send_weights(block, device, which=(0, 1, 2)):
        return [remote("t", weights_at(block)[n], weights_at(block)[n], device) for n in which]

    di_copies = [remote("t", di_of(blk(k)), di.at[di_part, own_cols], tpeer(k)) for k in range(1, 8)]
    weights_z = [send_weights(t, zpeer(k), (0, 2)) for k in (1, 3, 2)]
    load_dtab = local(dtab_ref, dtab)
    load_w = local(wqkv_ref, wv)
    next_table()
    for k in (1, 3, 2):
        code_copies[k].wait_recv()
        encode(k)
        if k == 3:
            next_table()
    tab_s.wait_recv()

    part_copies = {}
    tok_copies = {}

    def partial(j):
        cols = slice(starts[j], starts[j + 1])
        tab_x[j].wait_recv()
        forward = remote("r", tab.at[:, 2, :, chunk(j)], tab.at[:, 3, :, chunk(j)], sib)
        forward.wait_recv()
        table = tab[:, :, :, cols].reshape(2048, starts[j + 1] - starts[j])
        for k in (2, 1, 3, 0):
            part = dot(hot[k], table)
            if k == 0:
                emb[:, cols] += part
            else:
                psend[k, :, cols] = part.astype(BF16)
                part_copies[j, k] = remote(
                    "y", psend.at[k, :, chunk(j)], prec.at[4 - k, :, chunk(j)], ypeer(4 - k)
                )

    def send_tokens(h, j, slot):
        for k in (1, 3, 2):
            tok_copies[h, j, 2 * k + slot] = remote(
                "t", toks.at[slot, h, :, chunk(j)], toks.at[2 * k + slot, h, :, chunk(j)], zpeer(k)
            )

    def own(h, j):
        tok_copies[h, j, 1] = remote(
            "t", toks.at[0, h, :, chunk(j)], toks.at[1, h, :, chunk(j)], hpeer
        )
        send_tokens(h, j, 0)

    def relay(h, j):
        tok_copies[h, j, 1].wait_recv()
        send_tokens(h, j, 1)

    def settle(j):
        cols = slice(starts[j], starts[j + 1])
        for k in (1, 3, 2):
            part_copies[j, k].wait_recv()
        total = emb[:, cols]
        for k in (1, 2, 3):
            total = total + prec[k, :, cols].astype(F32)
        toks[0, :, :, cols] = total.astype(BF16).reshape(2, HR, -1)
        own(0, j)

    partial(0)
    next_table()
    partial(1)
    partial(2)
    settle(0)
    partial(3)
    settle(1)
    relay(0, 0)
    own(1, 0)
    mate = 2 * z + 1 - xh
    weights_x = send_weights(t, hpeer)
    settle(2)
    relay(0, 1)
    own(1, 1)
    settle(3)
    relay(0, 2)
    relay(1, 0)
    relay(0, 3)
    relay(1, 1)
    own(1, 2)
    own(1, 3)
    relay(1, 2)
    relay(1, 3)

    load_di.wait()
    for copy in di_copies:
        copy.wait_recv()
    di_y = [remote("y", di.at[di_part], di.at[di_part], ypeer(k)) for k in (1, 3, 2)]

    load_dtab.wait()
    entry = iota((1, 1024), 1).astype(F32)
    for b in range(7):
        onehot = jnp.where(colt[0, :, b : b + 1] == entry, 1.0, 0.0).astype(BF16)
        lk[b] = dot(onehot, dtab[b]).astype(BF16).reshape(2, HR, 128)
    lkf[:, :, :, own_cols] = lk[:, :, pl.ds(pl.multiple_of(HALF * t, HALF), HALF)]

    base_cos = bases_ref[0, pl.ds(s, 1), :]
    base_sin = bases_ref[1, pl.ds(s, 1), :]
    song_lanes = jnp.transpose(colt[0])[9:10, :]
    song_row = iota((16, HEAD), 0)

    def project(h):
        ssq = jnp.zeros((HR, 1), F32)
        for n, slot in enumerate((0, 1, 2, 6, 4, 3, 7, 5)):
            if slot:
                for j in range(4):
                    if slot > 1:
                        tok_copies[h, j, slot].wait_recv()
            feature = 2 * lax.rem(z + 4 - slot // 2, 4) + lax.rem(xh + slot % 2, 2)
            block = toks[slot, h].astype(F32)
            ssq = ssq + jnp.sum(block * block, axis=1, keepdims=True)
            place = pl.ds(pl.multiple_of(512 * feature, 512), 512)
            scaled = (block * again_ref[:, place]).astype(BF16)
            for i in range(3):
                product = dot(scaled, wv[i, place, :])
                if n == 0:
                    acc[i] = product
                else:
                    acc[i] += product
        factor = lax.rsqrt(ssq * (1.0 / 4096) + 1e-05)
        rows = slice(HR * h, HR * (h + 1))
        cosines = rows_ref[0, rows] * base_cos - rows_ref[1, rows] * base_sin
        sines = rows_ref[1, rows] * base_cos + rows_ref[0, rows] * base_sin
        sines = jnp.where(iota((1, HEAD), 1) < 64, -sines, sines)
        song_rows = jnp.where(song_row == 0, song_lanes[:, rows], 0.0).astype(BF16)
        for g in range(4):
            cols = slice(HEAD * g, HEAD * (g + 1))
            for i, start in ((0, 2 * HR + 16), (1, 0), (2, HR)):
                entries = acc[i, :, cols] * factor
                if i < 2:
                    entries = entries * cosines + pltpu.roll(entries, 64, 1) * sines
                kvs[h, g, start : start + HR, :] = entries.astype(BF16)
            kvs[h, g, 2 * HR : 2 * HR + 16, :] = song_rows

    kv_copies = {}
    kv_x = {}
    kv_s = {}
    kv_f = {}
    shared = pl.ds(0, 2 * HR + 16)

    def over_y(h):
        for k in (1, 3, 2):
            kv_copies[h, k] = remote(
                "y", kvs.at[h, lax.rem(y + k, 4)], kvb.at[h, 0, k], ypeer(k)
            )
        kvb[h, 0, 0] = kvs[h, y]

    def over_row(h):
        for k in (0, 1, 3, 2):
            if k:
                kv_copies[h, k].wait_recv()
            kv_x[h, k] = remote("r", kvb.at[h, 0, k, shared], kvb.at[h, 2, k, shared], xpeer)
            kv_s[h, k] = remote("r", kvb.at[h, 0, k, shared], kvb.at[h, 1, k, shared], sib)

    def over_cores(h):
        for k in (0, 1, 3, 2):
            kv_x[h, k].wait_recv()
            kv_f[h, k] = remote("r", kvb.at[h, 2, k, shared], kvb.at[h, 3, k, shared], sib)

    load_w.wait()
    project(0)
    over_y(0)
    over_row(0)
    project(1)
    over_y(1)

    for copy in weights_x:
        copy.wait_recv()
    weights_zq = [send_weights(mate, zpeer(k), (0,)) for k in (1, 3, 2)]
    weights_zx = [send_weights(mate, zpeer(k), (1, 2)) for k in (1, 3, 2)]
    weights_zv = [send_weights(t, zpeer(k), (1,)) for k in (1, 3, 2)]
    load_wout = [
        local(wout_ref.at[:, pl.ds(512 * j, 512)], wv.at[0, pl.ds(512 * j, 512)]) for j in range(8)
    ]
    over_cores(0)
    over_row(1)

    lk_copies = [
        remote(
            "t",
            lk.at[:, :, pl.ds(pl.multiple_of(HALF * blk(k), HALF), HALF)],
            lkf.at[:, :, :, own_cols],
            tpeer(k),
        )
        for k in range(1, 8)
    ]

    for copies in weights_z + weights_zq:
        for copy in copies:
            copy.wait_recv()
    dq_y = [remote("y", dq.at[0:2, dq_part], dq.at[0:2, dq_part], ypeer(k)) for k in (1, 3, 2)]

    over_cores(1)
    for h in range(2):
        for k in (0, 1, 3, 2):
            kv_s[h, k].wait_recv()
            kv_f[h, k].wait_recv()

    scale = HEAD**-0.5 * float(np.log2(np.e))
    key_lane = iota((HR, FR), 1)
    query_row = iota((HR, FR), 0)
    behind = (
        OWN * ((key_lane % HR) // HALF) + HALF * (key_lane // HR) + key_lane % HALF
    ) - (OWN * (query_row // HALF) + query_row % HALF)
    head_cols = pl.ds(pl.multiple_of(HEAD * y, HEAD), HEAD)
    o_copies = {}

    def attend(half, kq):
        yq = lax.rem(y + 4 - kq, 4)
        earlier = jnp.minimum(yq, 2)
        queries = kvb[half, 0, kq, 2 * HR + 16 :, :]
        query_song = jnp.broadcast_to(
            colt[kq, HR * half : HR * (half + 1), 9:10], (HR, HEAD)
        )

        def highest_of(group, highest, same_row):
            kk = lax.rem(kq + group, 4)
            for r in range(4):
                keys = jnp.concatenate([kvb[0, r, kk, :HR, :], kvb[1, r, kk, :HR, :]], axis=0)
                found = lax.dot_general(
                    queries, keys, (((1,), (1,)), ((), ())), preferred_element_type=F32
                )
                songs = [kvb[h, r, kk, 2 * HR : 2 * HR + 16, :].astype(F32)[0:1] for h in range(2)]
                allowed = jnp.concatenate([query_song == song for song in songs], axis=1)
                if same_row:
                    allowed = allowed & (behind <= FR * (q4 - ring(r)) + HALF * half)
                found = jnp.where(allowed, found, -1e30)
                sbuf[4 * group + r] = found
                highest = jnp.maximum(highest, jnp.maximum(found[:, :HEAD], found[:, HEAD:]))
            return highest

        highest = highest_of(0, jnp.full((HR, HEAD), -1e30, F32), True)
        highest = lax.fori_loop(
            1, earlier + 1, lambda group, carry: highest_of(group, carry, False), highest
        )
        peak = jnp.max(highest, axis=1, keepdims=True) * scale

        def blend(group, carry):
            totals, blended = carry
            kk = lax.rem(kq + group, 4)
            for r in range(4):
                weights = jnp.exp2(sbuf[4 * group + r] * scale - peak)
                totals = totals + (weights[:, :HEAD] + weights[:, HEAD:])
                held = jnp.concatenate(
                    [kvb[0, r, kk, HR : 2 * HR, :], kvb[1, r, kk, HR : 2 * HR, :]], axis=0
                )
                blended = blended + dot(weights.astype(BF16), held)
            return totals, blended

        totals, blended = lax.fori_loop(
            0, earlier + 1, blend, (jnp.zeros((HR, HEAD), F32), jnp.zeros((HR, HEAD), F32))
        )
        result = (blended / jnp.sum(totals, axis=1, keepdims=True)).astype(BF16)
        if kq:
            ob[half, kq] = result
            o_copies[half, kq] = remote(
                "y", ob.at[half, kq], att.at[half, :, head_cols], ypeer(4 - kq)
            )
        else:
            att[half, :, head_cols] = result

    for half in range(2):
        for kq in (2, 1, 3, 0):
            attend(half, kq)

    for copy in load_wout:
        copy.wait()
    r_copies = {}

    def columns_of(k, d):
        block = 2 * lax.rem(z + k, 4) + lax.rem(xh + d, 2)
        return wv[0, pl.ds(pl.multiple_of(512 * block, 512), 512), :]

    def send_sum(h, slot, value, device):
        rsend[h, slot] = value.astype(BF16)
        r_copies[h, slot] = remote("t", rsend.at[h, slot], rrec.at[h, slot], device)

    def arrived(h, slot):
        r_copies[h, slot].wait_recv()
        return rrec[h, slot].astype(F32)

    for k in (1, 2, 3):
        o_copies[0, k].wait_recv()
    for k in (2, 1, 3, 0):
        send_sum(0, k, dot(att[0], columns_of(k, 1)), hpeer)
    for k in (1, 2, 3):
        o_copies[1, k].wait_recv()
    for d in (1, 0):
        for k in (2, 1, 3):
            send_sum(1, 2 * k + d, dot(att[1], columns_of(k, d)), zpeer(k))
        if d:
            leave(*[r_copies[1, 2 * k + 1] for k in (2, 1, 3)])
    passed = dot(att[1], columns_of(0, 1))
    for k in (1, 3, 2):
        passed = passed + arrived(1, 2 * k + 1)
    send_sum(1, 1, passed, hpeer)
    for k in (2, 1, 3):
        send_sum(0, 4 + k, dot(att[0], columns_of(k, 0)) + arrived(0, k), zpeer(k))
    for h in range(2):
        resid[h] = toks[0, h].astype(F32) + dot(att[h], columns_of(0, 0))

    for copies in weights_zx + weights_zv:
        for copy in copies:
            copy.wait_recv()
    for copy in di_y:
        copy.wait_recv()
    di_forward = remote("r", di.at[di_half], di.at[di_half], sib)
    dv_forward = remote("r", dq.at[2, dq_half], dq.at[2, dq_half], sib)
    dp_forward = remote("r", dp.at[:, c], dp.at[:, c], sib)

    p_copies = {}
    th_copies = []
    place = iota((HR, HEAD), 1)

    def hand_over(h):
        total = resid[h]
        for slot in (2, 4, 6, 1) if h else (0, 5, 7, 6):
            total = total + arrived(h, slot)
        thl[h] = total.astype(BF16)
        hidden = thl[h].astype(F32)
        square = jnp.sum(hidden * hidden, axis=1, keepdims=True)
        high = square.astype(BF16).astype(F32)
        middle = (square - high).astype(BF16).astype(F32)
        low = square - high - middle
        squares = jnp.where(
            place == 0, high, jnp.where(place == 1, middle, jnp.where(place == 2, low, 0.0))
        )
        pfull[h, :, :, 1024:] = squares.astype(BF16).reshape(8, HALF, HEAD)
        gain = ogain_ref[:, pl.ds(pl.multiple_of(512 * t, 512), 512)]
        scaled = (hidden * gain).astype(BF16)
        if h:
            di_forward.wait_recv()
        pfull[h, :, :, :1024] = dot(scaled, di[...]).astype(BF16).reshape(8, HALF, 1024)
        for k in range(1, 8):
            p_copies[h, k] = remote("t", pfull.at[h, blk(k)], prb.at[h, k], tpeer(k))
        thb[h, :, pl.ds(pl.multiple_of(512 * t, 512), 512)] = thl[
            h, pl.ds(pl.multiple_of(HALF * t, HALF), HALF), :
        ]

    hand_over(1)
    hand_over(0)
    leave(*[p_copies[0, k] for k in range(1, 8)])
    for h in range(2):
        for k in range(1, 8):
            th_copies.append(
                remote(
                    "t",
                    thl.at[h, pl.ds(pl.multiple_of(HALF * blk(k), HALF), HALF)],
                    thb.at[h, :, pl.ds(pl.multiple_of(512 * t, 512), 512)],
                    tpeer(k),
                )
            )
    for copy in dq_y:
        copy.wait_recv()
    dq_forward = remote("r", dq.at[0:2, dq_half], dq.at[0:2, dq_half], sib)
    for copy in lk_copies:
        copy.wait_recv()

    left = iota((1, 128), 1) < DHEAD
    seen_row = iota((256, 128), 0) % 128
    seen_col = iota((256, 128), 1)
    seen = (seen_col <= seen_row) & (seen_col >= (seen_row // 8) * 8)
    out_row = iota((HR, HR), 0)
    order = jnp.where(
        iota((HR, HR), 1) == (out_row % 8) * HALF + out_row // 8, 1.0, 0.0
    ).astype(BF16)
    zero = jnp.zeros((), BF16)

    def depth(h):
        summed = pfull[h, t].astype(F32)
        for k in range(1, 8):
            p_copies[h, k].wait_recv()
            summed = summed + prb[h, k].astype(F32)
        square = jnp.sum(summed[:, 1024:], axis=1, keepdims=True)
        projected = summed[:, :1024] * lax.rsqrt(square * (1.0 / 4096) + 1e-05)
        inputs = [projected.astype(BF16)]
        for b in range(7):
            inputs.append((projected + lkf[b, h].astype(F32)).astype(BF16))
        inputs = dot(order, jnp.concatenate(inputs, axis=0))
        factor = lax.rsqrt(jnp.mean(inputs * inputs, axis=1, keepdims=True) + 1e-05)
        normed = (inputs * factor * dgain_ref[...]).astype(BF16)
        projections = []
        for i in range(3):
            if h and i != 1:
                (dq_forward if i == 0 else dv_forward).wait_recv()
            projections.append(dot(normed, dq[i]).astype(BF16))
        depth_q, depth_k, depth_v = projections
        for p in range(8):
            cols = slice(128 * p, 128 * (p + 1))
            pair = depth_q[:, cols]
            both = jnp.concatenate(
                [jnp.where(left, pair, zero), jnp.where(left, zero, pair)], axis=0
            )
            found = lax.dot_general(
                both, depth_k[:, cols], (((1,), (1,)), ((), ())), preferred_element_type=F32
            )
            found = jnp.where(seen, found, -1e30)
            peak = jnp.max(found, axis=1, keepdims=True)
            weights = jnp.exp((found - peak) * DHEAD**-0.5)
            totals = jnp.sum(weights, axis=1, keepdims=True)
            blended = dot(weights.astype(BF16), depth_v[:, cols]) / totals
            mixed[:, cols] = jnp.where(left, blended[:128], blended[128:]).astype(BF16)
        if h:
            dp_forward.wait_recv()
        dh_out[HR * h : HR * (h + 1), :] = (
            inputs + dot(mixed[...], dp[...].reshape(1024, 1024))
        ).astype(BF16)

    depth(1)
    depth(0)
    for copy in th_copies:
        copy.wait_recv()
    th_out[...] = thb[...].reshape(OWN, 4096)
    for copy in pending:
        if not any(copy is other for other in left_already):
            copy.wait_send()


def shards(
    audio_codes,
    chroma_ids,
    song_ids,
    code_table,
    chroma_table,
    attention_gain,
    temporal_qkv,
    temporal_out,
    output_gain,
    depth_input,
    depth_table,
    depth_gain,
    depth_qkv,
    depth_proj,
):
    rows, bases = rotation_tables()
    vmem = pl.BlockSpec(memory_space=pltpu.VMEM)
    anywhere = pl.BlockSpec(memory_space=pl.ANY)
    temporal, depth = pl.pallas_call(
        kernel,
        out_shape=(
            jax.ShapeDtypeStruct((OWN, 4096), BF16),
            jax.ShapeDtypeStruct((FR, 1024), BF16),
        ),
        in_specs=[vmem] * 8 + [anywhere] * 8,
        out_specs=(vmem, vmem),
        scratch_shapes=[
            pltpu.VMEM((3, 4096, 512), BF16),
            pltpu.VMEM((8, 4, 64, 512), BF16),
            pltpu.VMEM((4, FR, 2048), BF16),
            pltpu.VMEM((256, 512), BF16),
            pltpu.VMEM((7, 1024, 128), BF16),
            pltpu.VMEM((7, 2, HR, 128), BF16),
            pltpu.VMEM((7, 2, HALF, 1024), BF16),
            pltpu.VMEM((4, 16, FR), jnp.int32),
            pltpu.VMEM((4, FR, 16), F32),
            pltpu.VMEM((FR, 512), F32),
            pltpu.VMEM((2, HR, 512), F32),
            pltpu.VMEM((4, FR, 512), BF16),
            pltpu.VMEM((4, FR, 512), BF16),
            pltpu.VMEM((8, 2, HR, 512), BF16),
            pltpu.VMEM((3, HR, 512), F32),
            pltpu.VMEM((2, 4, PIECE, HEAD), BF16),
            pltpu.VMEM((2, 4, 4, PIECE, HEAD), BF16),
            pltpu.VMEM((12, HR, FR), F32),
            pltpu.VMEM((2, 4, HR, HEAD), BF16),
            pltpu.VMEM((2, HR, 512), BF16),
            pltpu.VMEM((2, 8, HR, 512), BF16),
            pltpu.VMEM((2, 8, HR, 512), BF16),
            pltpu.VMEM((2, HR, 512), BF16),
            pltpu.VMEM((2, HALF, 4096), BF16),
            pltpu.VMEM((512, 1024), BF16),
            pltpu.VMEM((2, 8, HALF, 1152), BF16),
            pltpu.VMEM((2, 8, HALF, 1152), BF16),
            pltpu.VMEM((3, 1024, 1024), BF16),
            pltpu.VMEM((8, 2, 64, 1024), BF16),
            pltpu.VMEM((HR, 1024), BF16),
            pltpu.SemaphoreType.DMA((16,)),
            pltpu.SemaphoreType.DMA((33,)),
            pltpu.SemaphoreType.DMA((33,)),
            pltpu.SemaphoreType.DMA((37,)),
            pltpu.SemaphoreType.DMA((37,)),
            pltpu.SemaphoreType.DMA((133,)),
            pltpu.SemaphoreType.DMA((133,)),
        ],
        compiler_params=pltpu.CompilerParams(
            collective_id=0, has_side_effects=True, vmem_limit_bytes=60 * 1024 * 1024
        ),
        name="layer",
    )(
        audio_codes.T,
        chroma_ids[None],
        song_ids[None],
        attention_gain[None],
        output_gain[None],
        depth_gain[None],
        rows,
        bases,
        code_table,
        chroma_table,
        temporal_qkv,
        temporal_out,
        depth_input,
        depth_table,
        depth_qkv,
        depth_proj,
    )
    return temporal, depth.reshape(OWN, 8, 1024)


def solution(mesh):
    placed = (
        P("seq", None),
        P("seq"),
        P("seq"),
        P(None, "seq", "tensor"),
        P(None, "tensor"),
        P(),
        P(None, None, "tensor"),
        P("tensor", None),
        P(),
        P(None, "tensor"),
        P(None, None, "tensor"),
        P(),
        P(None, None, "tensor"),
        P("tensor", None),
    )
    return jax.shard_map(
        shards,
        mesh=mesh,
        in_specs=placed,
        out_specs=(P(("seq", "tensor"), None), P(("seq", "tensor"), None, None)),
        check_vma=False,
    )
```

```python
import functools

import jax
import jax.numpy as jnp
import numpy as np
from jax import lax
from jax.experimental import pallas as pl
from jax.experimental.pallas import tpu as pltpu
from jax.sharding import PartitionSpec as P

MESH = pl.DeviceIdType.MESH
F32 = jnp.float32
BF16 = jnp.bfloat16
HEAD = 128
DHEAD = 64
FR = 256
OWN = 32
HR = FR // 2
HALF = OWN // 2
PIECE = 3 * HR + 16


def rotation_tables():
    freq = 10000.0 ** (-(np.arange(64, dtype=np.float64) * 2.0 / HEAD))
    frames = np.arange(FR, dtype=np.float64).reshape(8, 2, HALF).transpose(1, 0, 2).reshape(FR)
    row = frames[:, None] * freq[None]
    base = np.arange(16, dtype=np.float64)[:, None] * FR * freq[None]
    wide = lambda entries: np.concatenate([entries, entries], axis=1)
    rows = np.stack([wide(np.cos(row)), wide(np.sin(row))])
    bases = np.stack([wide(np.cos(base)), wide(np.sin(base))])
    return rows.astype(np.float32), bases.astype(np.float32)


def dot(a, b):
    return jnp.dot(a, b, preferred_element_type=F32)


def iota(shape, axis):
    return lax.broadcasted_iota(jnp.int32, shape, axis)


def kernel(
    codes_ref,
    chroma_ids_ref,
    songs_ref,
    again_ref,
    ogain_ref,
    dgain_ref,
    rows_ref,
    bases_ref,
    ctab_ref,
    chroma_ref,
    wqkv_ref,
    wout_ref,
    din_ref,
    dtab_ref,
    dqkv_ref,
    dproj_ref,
    th_out,
    dh_out,
    wv,
    tab,
    hot,
    chroma,
    dtab,
    lk,
    lkf,
    cpb,
    colt,
    emb,
    resid,
    psend,
    prec,
    toks,
    acc,
    kvs,
    kvb,
    sbuf,
    ob,
    att,
    rsend,
    rrec,
    thl,
    thb,
    di,
    pfull,
    prb,
    dq,
    dp,
    mixed,
    lsem,
    ysend,
    yrecv,
    rowsend,
    rowrecv,
    tsend,
    trecv,
):
    s = lax.axis_index("seq")
    t = lax.axis_index("tensor")
    y = s // 4
    x = (s // 2) % 2
    c = s % 2
    q4 = s % 4

    def ypeer(k):
        return (lax.rem(y + k, 4) * 4 + q4, t)

    sib = (y * 4 + x * 2 + (1 - c), t)
    xpeer = (y * 4 + (1 - x) * 2 + c, t)

    def tpeer(k):
        return (s, lax.rem(t + k, 8))

    def blk(k):
        return lax.rem(t + k, 8)

    def ring(r):
        return 2 * lax.rem(x + r // 2, 2) + lax.rem(c + r % 2, 2)

    counts = {"l": 0, "y": 0, "r": 0, "t": 0}
    pending = []
    left_already = []

    def leave(*copies):
        for copy in copies:
            copy.wait_send()
            left_already.append(copy)

    def local(src, dst):
        n = counts["l"]
        counts["l"] += 1
        copy = pltpu.make_async_copy(src, dst, lsem.at[n])
        copy.start()
        return copy

    def remote(kind, src, dst, device):
        sends, recvs = {
            "y": (ysend, yrecv),
            "r": (rowsend, rowrecv),
            "t": (tsend, trecv),
        }[kind]
        n = counts[kind]
        counts[kind] += 1
        copy = pltpu.make_async_remote_copy(
            src_ref=src,
            dst_ref=dst,
            send_sem=sends.at[n],
            recv_sem=recvs.at[n],
            device_id=device,
            device_id_type=MESH,
        )
        copy.start()
        pending.append(copy)
        return copy

    z = t // 2
    xh = t % 2

    def zpeer(k):
        return (s, 2 * lax.rem(z + k, 4) + xh)

    hpeer = (s, 2 * z + 1 - xh)
    load_tab = local(ctab_ref, tab.at[:, 0])
    load_chroma = local(chroma_ref, chroma)
    own_cols = pl.ds(pl.multiple_of(128 * t, 128), 128)
    dq_half = pl.ds(pl.multiple_of(512 * c, 512), 512)
    dq_part = pl.ds(pl.multiple_of(512 * c + 128 * y, 128), 128)
    dp_half = pl.ds(pl.multiple_of(64 * c, 64), 64)
    di_half = pl.ds(pl.multiple_of(256 * c, 256), 256)
    di_part = pl.ds(pl.multiple_of(256 * c + 64 * y, 64), 64)

    def di_of(block):
        return din_ref.at[pl.ds(pl.multiple_of(512 * block + 256 * c + 64 * y, 64), 64)]

    load_di = local(di_of(t), di.at[di_part, own_cols])
    load_weights = [
        local(dqkv_ref.at[0:2, dq_part], dq.at[0:2, dq_part, own_cols]),
        local(dqkv_ref.at[2, dq_half], dq.at[2, dq_half, own_cols]),
        local(dproj_ref.at[dp_half], dp.at[t, c]),
    ]


    cpb[0] = jnp.concatenate(
        [codes_ref[...], chroma_ids_ref[...], songs_ref[...], jnp.zeros((6, FR), jnp.int32)], axis=0
    )

    barrier = pltpu.get_barrier_semaphore()
    greeted = [ypeer(k) for k in (1, 2, 3)] + [sib, xpeer] + [tpeer(k) for k in range(1, 8)]
    for device in greeted:
        pl.semaphore_signal(barrier, inc=1, device_id=device, device_id_type=MESH)
    def to_columns(k):
        columns = jnp.transpose(cpb[k].astype(F32))
        colt[k] = jnp.concatenate(
            [
                columns[OWN * o + HALF * h : OWN * o + HALF * (h + 1)]
                for h in range(2)
                for o in range(8)
            ],
            axis=0,
        )

    lane = iota((1, 256), 1)
    lane_q = 2 * lax.rem(x + lane // 128, 2) + lax.rem(c + (lane // 64) % 2, 2)
    entry_row = (256 * y + 64 * lane_q + lane % 64).astype(F32)
    def encode(k):
        to_columns(k)
        for b in range(8):
            hot[k, :, 256 * b : 256 * (b + 1)] = jnp.where(
                colt[k, :, b : b + 1] == entry_row, 1.0, 0.0
            ).astype(BF16)

    encode(0)
    load_chroma.wait()
    chroma_hot = jnp.where(
        colt[0, :, 8:9] == iota((1, 256), 1).astype(F32), 1.0, 0.0
    ).astype(BF16)
    emb[...] = dot(chroma_hot, chroma[...])

    for copy in load_weights:
        copy.wait()
    load_tab.wait()
    pl.semaphore_wait(barrier, len(greeted))

    starts = (0, 128, 256, 384, 512)
    chunk = lambda j: pl.ds(starts[j], starts[j + 1] - starts[j])
    code_copies = {k: remote("y", cpb.at[0], cpb.at[k], ypeer(k)) for k in (1, 3, 2)}
    tab_x = []

    def next_table():
        j = len(tab_x)
        if j:
            leave(tab_x[-1])
        tab_x.append(
            remote("r", tab.at[:, 0, :, chunk(j)], tab.at[:, 2, :, chunk(j)], xpeer)
        )

    next_table()
    tab_s = remote("r", tab.at[:, 0], tab.at[:, 1], sib)

    def weights_at(block):
        cols = pl.ds(pl.multiple_of(128 * block, 128), 128)
        return (dq.at[0:2, dq_part, cols], dq.at[2, dq_half, cols], dp.at[block, c])

    def send_weights(block, device, which=(0, 1, 2)):
        return [remote("t", weights_at(block)[n], weights_at(block)[n], device) for n in which]

    di_copies = [remote("t", di_of(blk(k)), di.at[di_part, own_cols], tpeer(k)) for k in range(1, 8)]
    weights_z = [send_weights(t, zpeer(k), (0, 2)) for k in (1, 3, 2)]
    load_dtab = local(dtab_ref, dtab)
    load_w = local(wqkv_ref, wv)
    next_table()
    for k in (1, 3, 2):
        code_copies[k].wait_recv()
        encode(k)
        if k == 3:
            next_table()
    tab_s.wait_recv()

    part_copies = {}
    tok_copies = {}

    def partial(j):
        cols = slice(starts[j], starts[j + 1])
        tab_x[j].wait_recv()
        forward = remote("r", tab.at[:, 2, :, chunk(j)], tab.at[:, 3, :, chunk(j)], sib)
        forward.wait_recv()
        table = tab[:, :, :, cols].reshape(2048, starts[j + 1] - starts[j])
        for k in (2, 1, 3, 0):
            part = dot(hot[k], table)
            if k == 0:
                emb[:, cols] += part
            else:
                psend[k, :, cols] = part.astype(BF16)
                part_copies[j, k] = remote(
                    "y", psend.at[k, :, chunk(j)], prec.at[4 - k, :, chunk(j)], ypeer(4 - k)
                )

    def send_tokens(h, j, slot):
        for k in (1, 3, 2):
            tok_copies[h, j, 2 * k + slot] = remote(
                "t", toks.at[slot, h, :, chunk(j)], toks.at[2 * k + slot, h, :, chunk(j)], zpeer(k)
            )

    def own(h, j):
        tok_copies[h, j, 1] = remote(
            "t", toks.at[0, h, :, chunk(j)], toks.at[1, h, :, chunk(j)], hpeer
        )
        send_tokens(h, j, 0)

    def relay(h, j):
        tok_copies[h, j, 1].wait_recv()
        send_tokens(h, j, 1)

    def settle(j):
        cols = slice(starts[j], starts[j + 1])
        for k in (1, 3, 2):
            part_copies[j, k].wait_recv()
        total = emb[:, cols]
        for k in (1, 2, 3):
            total = total + prec[k, :, cols].astype(F32)
        toks[0, :, :, cols] = total.astype(BF16).reshape(2, HR, -1)
        own(0, j)

    partial(0)
    next_table()
    partial(1)
    partial(2)
    settle(0)
    partial(3)
    settle(1)
    relay(0, 0)
    own(1, 0)
    mate = 2 * z + 1 - xh
    weights_x = send_weights(t, hpeer)
    settle(2)
    relay(0, 1)
    own(1, 1)
    settle(3)
    relay(0, 2)
    relay(1, 0)
    relay(0, 3)
    relay(1, 1)
    own(1, 2)
    own(1, 3)
    relay(1, 2)
    relay(1, 3)

    load_di.wait()
    for copy in di_copies:
        copy.wait_recv()
    di_y = [remote("y", di.at[di_part], di.at[di_part], ypeer(k)) for k in (1, 3, 2)]

    load_dtab.wait()
    entry = iota((1, 1024), 1).astype(F32)
    for b in range(7):
        onehot = jnp.where(colt[0, :, b : b + 1] == entry, 1.0, 0.0).astype(BF16)
        lk[b] = dot(onehot, dtab[b]).astype(BF16).reshape(2, HR, 128)
    lkf[:, :, :, own_cols] = lk[:, :, pl.ds(pl.multiple_of(HALF * t, HALF), HALF)]

    base_cos = bases_ref[0, pl.ds(s, 1), :]
    base_sin = bases_ref[1, pl.ds(s, 1), :]
    song_lanes = jnp.transpose(colt[0])[9:10, :]
    song_row = iota((16, HEAD), 0)

    def project(h):
        ssq = jnp.zeros((HR, 1), F32)
        for n, slot in enumerate((0, 1, 2, 6, 4, 3, 7, 5)):
            if slot:
                for j in range(4):
                    if slot > 1:
                        tok_copies[h, j, slot].wait_recv()
            feature = 2 * lax.rem(z + 4 - slot // 2, 4) + lax.rem(xh + slot % 2, 2)
            block = toks[slot, h].astype(F32)
            ssq = ssq + jnp.sum(block * block, axis=1, keepdims=True)
            place = pl.ds(pl.multiple_of(512 * feature, 512), 512)
            scaled = (block * again_ref[:, place]).astype(BF16)
            for i in range(3):
                product = dot(scaled, wv[i, place, :])
                if n == 0:
                    acc[i] = product
                else:
                    acc[i] += product
        factor = lax.rsqrt(ssq * (1.0 / 4096) + 1e-05)
        rows = slice(HR * h, HR * (h + 1))
        cosines = rows_ref[0, rows] * base_cos - rows_ref[1, rows] * base_sin
        sines = rows_ref[1, rows] * base_cos + rows_ref[0, rows] * base_sin
        sines = jnp.where(iota((1, HEAD), 1) < 64, -sines, sines)
        song_rows = jnp.where(song_row == 0, song_lanes[:, rows], 0.0).astype(BF16)
        for g in range(4):
            cols = slice(HEAD * g, HEAD * (g + 1))
            for i, start in ((0, 2 * HR + 16), (1, 0), (2, HR)):
                entries = acc[i, :, cols] * factor
                if i < 2:
                    entries = entries * cosines + pltpu.roll(entries, 64, 1) * sines
                kvs[h, g, start : start + HR, :] = entries.astype(BF16)
            kvs[h, g, 2 * HR : 2 * HR + 16, :] = song_rows

    kv_copies = {}
    kv_x = {}
    kv_s = {}
    kv_f = {}
    shared = pl.ds(0, 2 * HR + 16)

    def over_y(h):
        for k in (1, 3, 2):
            kv_copies[h, k] = remote(
                "y", kvs.at[h, lax.rem(y + k, 4)], kvb.at[h, 0, k], ypeer(k)
            )
        kvb[h, 0, 0] = kvs[h, y]

    def over_row(h):
        for k in (0, 1, 3, 2):
            if k:
                kv_copies[h, k].wait_recv()
            kv_x[h, k] = remote("r", kvb.at[h, 0, k, shared], kvb.at[h, 2, k, shared], xpeer)
            kv_s[h, k] = remote("r", kvb.at[h, 0, k, shared], kvb.at[h, 1, k, shared], sib)

    def over_cores(h):
        for k in (0, 1, 3, 2):
            kv_x[h, k].wait_recv()
            kv_f[h, k] = remote("r", kvb.at[h, 2, k, shared], kvb.at[h, 3, k, shared], sib)

    load_w.wait()
    project(0)
    over_y(0)
    over_row(0)
    project(1)
    over_y(1)

    for copy in weights_x:
        copy.wait_recv()
    weights_zq = [send_weights(mate, zpeer(k), (0,)) for k in (1, 3, 2)]
    weights_zx = [send_weights(mate, zpeer(k), (1, 2)) for k in (1, 3, 2)]
    weights_zv = [send_weights(t, zpeer(k), (1,)) for k in (1, 3, 2)]
    load_wout = [
        local(wout_ref.at[:, pl.ds(512 * j, 512)], wv.at[0, pl.ds(512 * j, 512)]) for j in range(8)
    ]
    over_cores(0)
    over_row(1)

    lk_copies = [
        remote(
            "t",
            lk.at[:, :, pl.ds(pl.multiple_of(HALF * blk(k), HALF), HALF)],
            lkf.at[:, :, :, own_cols],
            tpeer(k),
        )
        for k in range(1, 8)
    ]

    over_cores(1)

    for copies in weights_z + weights_zq:
        for copy in copies:
            copy.wait_recv()
    dq_y = [remote("y", dq.at[0:2, dq_part], dq.at[0:2, dq_part], ypeer(k)) for k in (1, 3, 2)]

    for h in range(2):
        for k in (0, 1, 3, 2):
            kv_s[h, k].wait_recv()
            kv_f[h, k].wait_recv()

    scale = HEAD**-0.5 * float(np.log2(np.e))
    key_lane = iota((HR, FR), 1)
    query_row = iota((HR, FR), 0)
    behind = (
        OWN * ((key_lane % HR) // HALF) + HALF * (key_lane // HR) + key_lane % HALF
    ) - (OWN * (query_row // HALF) + query_row % HALF)
    head_cols = pl.ds(pl.multiple_of(HEAD * y, HEAD), HEAD)
    o_copies = {}

    def attend(half, kq):
        yq = lax.rem(y + 4 - kq, 4)
        earlier = jnp.minimum(yq, 2)
        queries = kvb[half, 0, kq, 2 * HR + 16 :, :]
        query_song = jnp.broadcast_to(
            colt[kq, HR * half : HR * (half + 1), 9:10], (HR, HEAD)
        )

        def highest_of(group, highest, same_row):
            kk = lax.rem(kq + group, 4)
            for r in range(4):
                keys = jnp.concatenate([kvb[0, r, kk, :HR, :], kvb[1, r, kk, :HR, :]], axis=0)
                found = lax.dot_general(
                    queries, keys, (((1,), (1,)), ((), ())), preferred_element_type=F32
                )
                songs = [kvb[h, r, kk, 2 * HR : 2 * HR + 16, :].astype(F32)[0:1] for h in range(2)]
                allowed = jnp.concatenate([query_song == song for song in songs], axis=1)
                if same_row:
                    allowed = allowed & (behind <= FR * (q4 - ring(r)) + HALF * half)
                found = jnp.where(allowed, found, -1e30)
                sbuf[4 * group + r] = found
                highest = jnp.maximum(highest, jnp.maximum(found[:, :HEAD], found[:, HEAD:]))
            return highest

        highest = highest_of(0, jnp.full((HR, HEAD), -1e30, F32), True)
        highest = lax.fori_loop(
            1, earlier + 1, lambda group, carry: highest_of(group, carry, False), highest
        )
        peak = jnp.max(highest, axis=1, keepdims=True) * scale

        def blend(group, carry):
            totals, blended = carry
            kk = lax.rem(kq + group, 4)
            for r in range(4):
                weights = jnp.exp2(sbuf[4 * group + r] * scale - peak)
                totals = totals + (weights[:, :HEAD] + weights[:, HEAD:])
                held = jnp.concatenate(
                    [kvb[0, r, kk, HR : 2 * HR, :], kvb[1, r, kk, HR : 2 * HR, :]], axis=0
                )
                blended = blended + dot(weights.astype(BF16), held)
            return totals, blended

        totals, blended = lax.fori_loop(
            0, earlier + 1, blend, (jnp.zeros((HR, HEAD), F32), jnp.zeros((HR, HEAD), F32))
        )
        result = (blended / jnp.sum(totals, axis=1, keepdims=True)).astype(BF16)
        if kq:
            ob[half, kq] = result
            o_copies[half, kq] = remote(
                "y", ob.at[half, kq], att.at[half, :, head_cols], ypeer(4 - kq)
            )
        else:
            att[half, :, head_cols] = result

    for half in range(2):
        for kq in (2, 1, 3, 0):
            attend(half, kq)

    for copy in load_wout:
        copy.wait()
    r_copies = {}

    def columns_of(k, d):
        block = 2 * lax.rem(z + k, 4) + lax.rem(xh + d, 2)
        return wv[0, pl.ds(pl.multiple_of(512 * block, 512), 512), :]

    def send_sum(h, slot, value, device):
        rsend[h, slot] = value.astype(BF16)
        r_copies[h, slot] = remote("t", rsend.at[h, slot], rrec.at[h, slot], device)

    def arrived(h, slot):
        r_copies[h, slot].wait_recv()
        return rrec[h, slot].astype(F32)

    for k in (1, 2, 3):
        o_copies[0, k].wait_recv()
    for k in (2, 1, 3, 0):
        send_sum(0, k, dot(att[0], columns_of(k, 1)), hpeer)
    for k in (1, 2, 3):
        o_copies[1, k].wait_recv()
    for d in (1, 0):
        for k in (2, 1, 3):
            send_sum(1, 2 * k + d, dot(att[1], columns_of(k, d)), zpeer(k))
        if d:
            leave(*[r_copies[1, 2 * k + 1] for k in (2, 1, 3)])
    passed = dot(att[1], columns_of(0, 1))
    for k in (1, 3, 2):
        passed = passed + arrived(1, 2 * k + 1)
    send_sum(1, 1, passed, hpeer)
    for k in (2, 1, 3):
        send_sum(0, 4 + k, dot(att[0], columns_of(k, 0)) + arrived(0, k), zpeer(k))
    for h in range(2):
        resid[h] = toks[0, h].astype(F32) + dot(att[h], columns_of(0, 0))

    for copies in weights_zx + weights_zv:
        for copy in copies:
            copy.wait_recv()
    for copy in di_y:
        copy.wait_recv()
    di_forward = remote("r", di.at[di_half], di.at[di_half], sib)
    dv_forward = remote("r", dq.at[2, dq_half], dq.at[2, dq_half], sib)
    dp_forward = remote("r", dp.at[:, c], dp.at[:, c], sib)

    p_copies = {}
    th_copies = []
    place = iota((HR, HEAD), 1)

    def hand_over(h):
        total = resid[h]
        for slot in (2, 4, 6, 1) if h else (0, 5, 7, 6):
            total = total + arrived(h, slot)
        thl[h] = total.astype(BF16)
        hidden = thl[h].astype(F32)
        square = jnp.sum(hidden * hidden, axis=1, keepdims=True)
        high = square.astype(BF16).astype(F32)
        middle = (square - high).astype(BF16).astype(F32)
        low = square - high - middle
        squares = jnp.where(
            place == 0, high, jnp.where(place == 1, middle, jnp.where(place == 2, low, 0.0))
        )
        pfull[h, :, :, 1024:] = squares.astype(BF16).reshape(8, HALF, HEAD)
        gain = ogain_ref[:, pl.ds(pl.multiple_of(512 * t, 512), 512)]
        scaled = (hidden * gain).astype(BF16)
        if h:
            di_forward.wait_recv()
        pfull[h, :, :, :1024] = dot(scaled, di[...]).astype(BF16).reshape(8, HALF, 1024)
        for k in range(1, 8):
            p_copies[h, k] = remote("t", pfull.at[h, blk(k)], prb.at[h, k], tpeer(k))
        thb[h, :, pl.ds(pl.multiple_of(512 * t, 512), 512)] = thl[
            h, pl.ds(pl.multiple_of(HALF * t, HALF), HALF), :
        ]

    hand_over(1)
    hand_over(0)
    for copy in dq_y:
        copy.wait_recv()
    dq_forward = remote("r", dq.at[0:2, dq_half], dq.at[0:2, dq_half], sib)
    leave(*[p_copies[0, k] for k in range(1, 8)])
    for h in range(2):
        for k in range(1, 8):
            th_copies.append(
                remote(
                    "t",
                    thl.at[h, pl.ds(pl.multiple_of(HALF * blk(k), HALF), HALF)],
                    thb.at[h, :, pl.ds(pl.multiple_of(512 * t, 512), 512)],
                    tpeer(k),
                )
            )
    for copy in lk_copies:
        copy.wait_recv()

    left = iota((1, 128), 1) < DHEAD
    seen_row = iota((256, 128), 0) % 128
    seen_col = iota((256, 128), 1)
    seen = (seen_col <= seen_row) & (seen_col >= (seen_row // 8) * 8)
    out_row = iota((HR, HR), 0)
    order = jnp.where(
        iota((HR, HR), 1) == (out_row % 8) * HALF + out_row // 8, 1.0, 0.0
    ).astype(BF16)
    zero = jnp.zeros((), BF16)

    def depth(h):
        summed = pfull[h, t].astype(F32)
        for k in range(1, 8):
            p_copies[h, k].wait_recv()
            summed = summed + prb[h, k].astype(F32)
        square = jnp.sum(summed[:, 1024:], axis=1, keepdims=True)
        projected = summed[:, :1024] * lax.rsqrt(square * (1.0 / 4096) + 1e-05)
        inputs = [projected.astype(BF16)]
        for b in range(7):
            inputs.append((projected + lkf[b, h].astype(F32)).astype(BF16))
        inputs = dot(order, jnp.concatenate(inputs, axis=0))
        factor = lax.rsqrt(jnp.mean(inputs * inputs, axis=1, keepdims=True) + 1e-05)
        normed = (inputs * factor * dgain_ref[...]).astype(BF16)
        projections = []
        for i in range(3):
            if h and i != 1:
                (dq_forward if i == 0 else dv_forward).wait_recv()
            projections.append(dot(normed, dq[i]).astype(BF16))
        depth_q, depth_k, depth_v = projections
        for p in range(8):
            cols = slice(128 * p, 128 * (p + 1))
            pair = depth_q[:, cols]
            both = jnp.concatenate(
                [jnp.where(left, pair, zero), jnp.where(left, zero, pair)], axis=0
            )
            found = lax.dot_general(
                both, depth_k[:, cols], (((1,), (1,)), ((), ())), preferred_element_type=F32
            )
            found = jnp.where(seen, found, -1e30)
            peak = jnp.max(found, axis=1, keepdims=True)
            weights = jnp.exp((found - peak) * DHEAD**-0.5)
            totals = jnp.sum(weights, axis=1, keepdims=True)
            blended = dot(weights.astype(BF16), depth_v[:, cols]) / totals
            mixed[:, cols] = jnp.where(left, blended[:128], blended[128:]).astype(BF16)
        if h:
            dp_forward.wait_recv()
        dh_out[HR * h : HR * (h + 1), :] = (
            inputs + dot(mixed[...], dp[...].reshape(1024, 1024))
        ).astype(BF16)

    depth(1)
    depth(0)
    for copy in th_copies:
        copy.wait_recv()
    th_out[...] = thb[...].reshape(OWN, 4096)
    for copy in pending:
        if not any(copy is other for other in left_already):
            copy.wait_send()


def shards(
    audio_codes,
    chroma_ids,
    song_ids,
    code_table,
    chroma_table,
    attention_gain,
    temporal_qkv,
    temporal_out,
    output_gain,
    depth_input,
    depth_table,
    depth_gain,
    depth_qkv,
    depth_proj,
):
    rows, bases = rotation_tables()
    vmem = pl.BlockSpec(memory_space=pltpu.VMEM)
    anywhere = pl.BlockSpec(memory_space=pl.ANY)
    temporal, depth = pl.pallas_call(
        kernel,
        out_shape=(
            jax.ShapeDtypeStruct((OWN, 4096), BF16),
            jax.ShapeDtypeStruct((FR, 1024), BF16),
        ),
        in_specs=[vmem] * 8 + [anywhere] * 8,
        out_specs=(vmem, vmem),
        scratch_shapes=[
            pltpu.VMEM((3, 4096, 512), BF16),
            pltpu.VMEM((8, 4, 64, 512), BF16),
            pltpu.VMEM((4, FR, 2048), BF16),
            pltpu.VMEM((256, 512), BF16),
            pltpu.VMEM((7, 1024, 128), BF16),
            pltpu.VMEM((7, 2, HR, 128), BF16),
            pltpu.VMEM((7, 2, HALF, 1024), BF16),
            pltpu.VMEM((4, 16, FR), jnp.int32),
            pltpu.VMEM((4, FR, 16), F32),
            pltpu.VMEM((FR, 512), F32),
            pltpu.VMEM((2, HR, 512), F32),
            pltpu.VMEM((4, FR, 512), BF16),
            pltpu.VMEM((4, FR, 512), BF16),
            pltpu.VMEM((8, 2, HR, 512), BF16),
            pltpu.VMEM((3, HR, 512), F32),
            pltpu.VMEM((2, 4, PIECE, HEAD), BF16),
            pltpu.VMEM((2, 4, 4, PIECE, HEAD), BF16),
            pltpu.VMEM((12, HR, FR), F32),
            pltpu.VMEM((2, 4, HR, HEAD), BF16),
            pltpu.VMEM((2, HR, 512), BF16),
            pltpu.VMEM((2, 8, HR, 512), BF16),
            pltpu.VMEM((2, 8, HR, 512), BF16),
            pltpu.VMEM((2, HR, 512), BF16),
            pltpu.VMEM((2, HALF, 4096), BF16),
            pltpu.VMEM((512, 1024), BF16),
            pltpu.VMEM((2, 8, HALF, 1152), BF16),
            pltpu.VMEM((2, 8, HALF, 1152), BF16),
            pltpu.VMEM((3, 1024, 1024), BF16),
            pltpu.VMEM((8, 2, 64, 1024), BF16),
            pltpu.VMEM((HR, 1024), BF16),
            pltpu.SemaphoreType.DMA((16,)),
            pltpu.SemaphoreType.DMA((33,)),
            pltpu.SemaphoreType.DMA((33,)),
            pltpu.SemaphoreType.DMA((37,)),
            pltpu.SemaphoreType.DMA((37,)),
            pltpu.SemaphoreType.DMA((133,)),
            pltpu.SemaphoreType.DMA((133,)),
        ],
        compiler_params=pltpu.CompilerParams(
            collective_id=0, has_side_effects=True, vmem_limit_bytes=60 * 1024 * 1024
        ),
        name="layer",
    )(
        audio_codes.T,
        chroma_ids[None],
        song_ids[None],
        attention_gain[None],
        output_gain[None],
        depth_gain[None],
        rows,
        bases,
        code_table,
        chroma_table,
        temporal_qkv,
        temporal_out,
        depth_input,
        depth_table,
        depth_qkv,
        depth_proj,
    )
    return temporal, depth.reshape(OWN, 8, 1024)


def solution(mesh):
    placed = (
        P("seq", None),
        P("seq"),
        P("seq"),
        P(None, "seq", "tensor"),
        P(None, "tensor"),
        P(),
        P(None, None, "tensor"),
        P("tensor", None),
        P(),
        P(None, "tensor"),
        P(None, None, "tensor"),
        P(),
        P(None, None, "tensor"),
        P("tensor", None),
    )
    return jax.shard_map(
        shards,
        mesh=mesh,
        in_specs=placed,
        out_specs=(P(("seq", "tensor"), None), P(("seq", "tensor"), None, None)),
        check_vma=False,
    )
```
